32 devices in a mesh: row: 2 (over core), col: 4 (over z), img: 4 (over y, x).
Axes of the slice: x: 2, y: 2, z: 4, core: 2. Of those that a mesh axis runs over, the one named last changes fastest.
Arguments:
- canvases: bfloat16 [8, 64, 64, 2048], P('img', 'row', 'col')
- layout: int32 [8], P('img'), may hold values from 0 to 1, as said below
- labels: int32 [8, 64, 64], P('img', 'row', 'col'), may hold values from 0 to 18
- branch_w: bfloat16 [2048, 4, 512], P(('row', 'col', 'img')), may hold values from -0.125 to 0.125
- branch_gain: float32 [4, 512], replicated, may hold values from 0.1 to 1.9
- branch_bias: float32 [4, 512], replicated, may hold values from -3 to 3
- join_w: bfloat16 [4096, 9, 512], P(('row', 'col', 'img')), may hold values from -0.03125 to 0.03125
- join_gain: float32 [512], replicated, may hold values from 0.1 to 1.9
- join_bias: float32 [512], replicated, may hold values from -3 to 3
- class_w: bfloat16 [512, 19], replicated, may hold values from -0.5 to 0.5
- class_bias: float32 [19], replicated, may hold values from -4 to 4
Outputs:
- logits: float32 [8, 64, 64, 19], P('img', 'row', 'col')
- grad_canvases: float32 [8, 64, 64, 2048], P('img', 'row', 'col')
- grad_branch_w: float32 [2048, 4, 512], P(('row', 'col', 'img'))
- grad_branch_gain: float32 [4, 512], replicated
- grad_branch_bias: float32 [4, 512], replicated
- grad_join_w: float32 [4096, 9, 512], P(('row', 'col', 'img'))
- grad_join_gain: float32 [512], replicated
- grad_join_bias: float32 [512], replicated
- grad_class_w: float32 [512, 19], replicated
- grad_class_bias: float32 [19], replicated
The draws below stay inside these ranges and needn't reach their ends.
Inputs may be any that keep to these rules, and one draw needn't show every extreme that they name: `layout`: 0 marks a canvas holding one image of 64 x 64 pixels, 1 a canvas holding four images of half that side in its quadrants; among each index of img's 2 canvases at least one is marked 0.
All inputs are finite; a program needn't handle non-finite values.
Results may differ from the reference program's by a relative error of at most 0.015.
Values may be sent and summed in bfloat16 or wider, within the bound.
No kernel may reach another device: no remote copies, remote signals or barrier semaphores. Data moves between devices by JAX's collectives and lax.ppermute only.
A program may use at most 576 MiB of HBM per device.

```python
import math
from functools import partial
import jax
import jax.numpy as jnp
from jax import lax

C = 2048
MID = 512
NCLS = 19
NBIN = 4
TAPS = 9
SIDE = 64
CAN_DEV = 2
CANVASES = 8
CAT = 4096
NPIX = 32768


def draw_canvases(key, part):
    key = jax.random.fold_in(key, 11)
    key_mean, key_noise = jax.random.split(key, 2)
    means = jax.random.normal(key_mean, (CANVASES, 2, 2, C), jnp.float32)
    noise = jax.random.normal(key_noise, (CANVASES, SIDE, SIDE, C), jnp.float32)
    spread_means = jnp.repeat(jnp.repeat(means, SIDE // 2, axis=1), SIDE // 2, axis=2)
    return jnp.clip(spread_means + noise, -8.0, 8.0).astype(jnp.bfloat16)


def draw_layout(key, part):
    key = jax.random.fold_in(key, 5)
    key_flags, key_picks = jax.random.split(key, 2)
    layouts = jax.random.randint(key_flags, (CANVASES,), 0, 2, jnp.int32)
    picks = jax.random.randint(key_picks, (CANVASES // CAN_DEV,), 0, CAN_DEV, jnp.int32)
    chosen = jnp.arange(CANVASES // CAN_DEV, dtype=jnp.int32) * CAN_DEV + picks
    return layouts.at[chosen].set(0)


def place_ends(array, stream_key, least, top_value):
    place = [jax.random.randint(jax.random.fold_in(stream_key, axis), (), 0, length) for axis, length in enumerate(array.shape)]
    widest = array.shape.index(max(array.shape))
    next_to = place[:widest] + [(place[widest] + 1) % array.shape[widest]] + place[widest + 1:]
    return array.at[tuple(place)].set(least).at[tuple(next_to)].set(top_value)


def level_of(key, extent, cuts, smallest, top_value):
    level, own = 1.0, jax.random.fold_in(key, 6)
    for position, parts in cuts:
        heights = jnp.exp(jax.random.uniform(jax.random.fold_in(own, position), (parts,), jnp.float32, smallest / len(cuts), top_value / len(cuts)))
        level = level * jnp.repeat(heights, extent[position] // parts).reshape([-1 if axis == position else 1 for axis in range(len(extent))])
    return level


def normal_values(key, extent, width, limit, shards=(), kind=jnp.bfloat16):
    gain = level_of(key, extent, shards, -0.22, 0.18) if shards else 1.0
    values = jax.random.normal(key, extent, jnp.float32) * width * gain
    return jnp.minimum(jnp.maximum(values, -limit), limit).astype(kind)


def setup_inputs(seed: int = 0) -> dict:
    key_list = jax.random.split(jax.random.key(seed), 12)
    canvases = draw_canvases(jax.random.fold_in(key_list[11], 71), 0)
    layout = draw_layout(jax.random.fold_in(key_list[11], 71), 0)
    labels = place_ends(jax.random.randint(key_list[2], (CANVASES, SIDE, SIDE), 0, NCLS), jax.random.fold_in(key_list[2], 1), 0, NCLS - 1).astype(jnp.int32)
    branch_w = normal_values(key_list[3], (C, NBIN, MID), C ** -0.5, 0.125, ((0, 32),))
    branch_gain = jnp.clip(1.0 + 0.18 * jax.random.normal(key_list[4], (NBIN, MID), jnp.float32), 0.1, 1.9)
    branch_bias = normal_values(key_list[5], (NBIN, MID), 0.5, 3.0, (), jnp.float32)
    join_w = normal_values(key_list[6], (CAT, TAPS, MID), (TAPS * CAT) ** -0.5, 0.03125, ((0, 32),))
    join_gain = jnp.clip(1.0 + 0.18 * jax.random.normal(key_list[7], (MID,), jnp.float32), 0.1, 1.9)
    join_bias = normal_values(key_list[8], (MID,), 0.5, 3.0, (), jnp.float32)
    class_w = normal_values(key_list[9], (MID, NCLS), (MID // 4) ** -0.5, 0.5)
    class_bias = normal_values(key_list[10], (NCLS,), 1.0, 4.0, (), jnp.float32)
    return {"canvases": canvases, "layout": layout, "labels": labels, "branch_w": branch_w, "branch_gain": branch_gain, "branch_bias": branch_bias, "join_w": join_w, "join_gain": join_gain, "join_bias": join_bias, "class_w": class_w, "class_bias": class_bias}


bin_scales = (1, 2, 3, 6)
epsilon = 1e-05

@jax.custom_vjp
def low(v):
    return lax.optimization_barrier(v.astype(jnp.bfloat16)).astype(jnp.float32)

@jax.custom_vjp
def low_back(v):
    return v

def low_keep(v):
    return (low(v), None)

def low_pass(kept, grad):
    return (grad,)

def back_keep(v):
    return (v, None)

def back_low(kept, grad):
    return (low(grad),)
low.defvjp(low_keep, low_pass)
low_back.defvjp(back_keep, back_low)

def axis_tables(layouts, coords, bin_size, canvas_side):
    packed = layouts[:, None, None]
    half_side = canvas_side // 2
    image_side = jnp.where(packed == 1, half_side, canvas_side)
    cell_ids = jnp.arange(2 * bin_size, dtype=jnp.int32)[None, :, None]
    which_half = cell_ids // bin_size
    in_cell = cell_ids % bin_size
    places = coords[None, None, :]
    pixel_half = jnp.where(packed == 1, places // half_side, 0)
    local_pos = places - pixel_half * image_side
    usable = (packed == 1) | (which_half == 0)
    same_image = (pixel_half == which_half) & usable
    low_edge = in_cell * image_side // bin_size
    high_edge = ((in_cell + 1) * image_side + bin_size - 1) // bin_size
    inside = same_image & (local_pos >= low_edge) & (local_pos < high_edge)
    numerator = local_pos * (bin_size - 1)
    base_cell = numerator // (image_side - 1)
    fraction = (numerator - base_cell * (image_side - 1)).astype(jnp.float32) / (image_side - 1).astype(jnp.float32)
    weight = jnp.where(in_cell == base_cell, 1.0 - fraction, 0.0) + jnp.where(in_cell == base_cell + 1, fraction, 0.0)
    weight = jnp.where(same_image, weight, 0.0)
    return (inside.astype(jnp.float32), weight, usable[:, :, 0].astype(jnp.float32))

def canvas_tables(layouts, rows_at, cols_at, bin_size, canvas_side):
    canvas_count = layouts.shape[0]
    pool_rows, up_rows, valid_rows = axis_tables(layouts, rows_at, bin_size, canvas_side)
    pool_cols, up_cols, valid_cols = axis_tables(layouts, cols_at, bin_size, canvas_side)
    all_places = jnp.arange(canvas_side, dtype=jnp.int32)
    per_axis = lax.optimization_barrier(jnp.sum(axis_tables(layouts, all_places, bin_size, canvas_side)[0], axis=2))
    cell_total = 4 * bin_size * bin_size
    pixel_total = rows_at.shape[0] * cols_at.shape[0]
    pool_table = (pool_rows[:, :, None, :, None] * pool_cols[:, None, :, None, :]).reshape(canvas_count, cell_total, pixel_total)
    up_table = (up_rows[:, :, None, :, None] * up_cols[:, None, :, None, :]).reshape(canvas_count, cell_total, pixel_total)
    counted = (per_axis[:, :, None] * per_axis[:, None, :]).reshape(canvas_count, cell_total)
    cell_mask = (valid_rows[:, :, None] * valid_cols[:, None, :]).reshape(canvas_count, cell_total)
    return (pool_table, up_table, counted, cell_mask)

def conv_canvas(image, kernel):
    padded = jnp.pad(image, ((1, 1), (1, 1), (0, 0)))
    total = jnp.zeros((SIDE, SIDE, MID), image.dtype)
    for tap_index in range(9):
        down_by = tap_index // 3
        right_by = tap_index % 3
        total = total + jnp.einsum('yxc,cm->yxm', padded[down_by:down_by + SIDE, right_by:right_by + SIDE], kernel[:, tap_index, :], precision=lax.Precision.HIGHEST)
    return total

def forward(tables, onehot, canvases, branch_w, branch_gain, branch_bias, join_w, join_gain, join_bias, class_w, class_bias):
    pool_all, up_list, count_all, mask_list = tables
    highest = lax.Precision.HIGHEST
    canvas_count = canvases.shape[0]
    flat_pixels = canvases.reshape(canvas_count, SIDE * SIDE, C)
    pool_sums = jnp.einsum('nkp,npc->nkc', pool_all, flat_pixels, precision=highest)
    pooled = low(pool_sums / jnp.maximum(count_all, 1.0)[:, :, None])
    pieces = [flat_pixels]
    first_cell = 0
    for bin_level, bin_size in enumerate(bin_scales):
        span_cells = 4 * bin_size * bin_size
        pre_norm = low_back(jnp.einsum('nkc,cm->nkm', pooled[:, first_cell:first_cell + span_cells], branch_w[:, bin_level, :], precision=highest))
        cell_mask = mask_list[bin_level][:, :, None]
        valid_count = jnp.sum(mask_list[bin_level])
        bin_mean = lax.optimization_barrier(jnp.sum(cell_mask * pre_norm, axis=(0, 1))) / valid_count
        bin_var = lax.optimization_barrier(jnp.sum(cell_mask * pre_norm * pre_norm, axis=(0, 1))) / valid_count - bin_mean * bin_mean
        normed = (pre_norm - bin_mean) * lax.rsqrt(bin_var + epsilon)
        feature = low(jax.nn.gelu(branch_gain[bin_level] * normed + branch_bias[bin_level]))
        lifted = jnp.einsum('nkp,nkm->npm', up_list[bin_level], feature, precision=highest)
        pieces.append(low_back(low(lifted)))
        first_cell += span_cells
    concat = jnp.concatenate(pieces, axis=2).reshape(canvas_count, SIDE, SIDE, CAT)
    per_canvas = jax.checkpoint(lambda image: conv_canvas(image, join_w))
    joined_out = low_back(lax.map(per_canvas, concat))
    head_mean = lax.optimization_barrier(jnp.mean(joined_out, axis=(0, 1, 2)))
    head_var = lax.optimization_barrier(jnp.mean(joined_out * joined_out, axis=(0, 1, 2))) - head_mean * head_mean
    normed_head = (joined_out - head_mean) * lax.rsqrt(head_var + epsilon)
    activated = low(jax.nn.gelu(join_gain * normed_head + join_bias))
    logits = low_back(jnp.einsum('nyxm,mk->nyxk', activated, class_w, precision=highest) + class_bias)
    pixel_loss = jax.scipy.special.logsumexp(logits, axis=-1) - lax.optimization_barrier(jnp.sum(logits * onehot, axis=-1))
    loss_value = jnp.sum(pixel_loss) / math.sqrt(NPIX)
    return (loss_value, logits)

def reference(canvases, layout, labels, branch_w, branch_gain, branch_bias, join_w, join_gain, join_bias, class_w, class_bias):
    all_places = jnp.arange(SIDE, dtype=jnp.int32)
    table_sets = [canvas_tables(layout, all_places, all_places, bin_size, SIDE) for bin_size in bin_scales]
    pool_all = jnp.concatenate([table_set[0] for table_set in table_sets], axis=1)
    up_list = [low(table_set[1]) for table_set in table_sets]
    count_all = jnp.concatenate([table_set[2] for table_set in table_sets], axis=1)
    mask_list = [table_set[3] for table_set in table_sets]
    onehot = (labels[..., None] == jnp.arange(NCLS, dtype=jnp.int32)).astype(jnp.float32)
    floats = tuple((value.astype(jnp.float32) for value in (canvases, branch_w, branch_gain, branch_bias, join_w, join_gain, join_bias, class_w, class_bias)))
    loss_value, pullback, logits = jax.vjp(partial(forward, (pool_all, up_list, count_all, mask_list), onehot), *floats, has_aux=True)
    gradients = pullback(jnp.ones_like(loss_value))
    return (logits, gradients[0], gradients[1], gradients[2], gradients[3], gradients[4], gradients[5], gradients[6], gradients[7], gradients[8])
```

```python
import functools
import math

import jax
import jax.numpy as jnp
import numpy as np
from jax import lax
from jax.sharding import PartitionSpec as P

SIDE = 64
bin_scales = (1, 2, 3, 6)
epsilon = 1e-05
LEVELS = len(bin_scales)
TAPS = 9
BF16 = jnp.bfloat16
F32 = jnp.float32


def slot_lists():
    rows = []
    for level, size in enumerate(bin_scales):
        rows += [(level, a, b, 0) for a in range(2 * size) for b in range(2 * size)]
    for level, size in enumerate(bin_scales):
        rows += [(level, a, b, 1) for a in range(size) for b in range(size)]
    rows += [(-1, 0, 0, 1)] * (-len(rows) % 128)
    return [np.array(column) for column in zip(*rows)]


def axis_tables(cell, level):
    size = np.array(bin_scales)[np.maximum(level, 0)][:, None]
    places = np.arange(SIDE)[None, :]
    pools, ups, valids = [], [], []
    for packed in (0, 1):
        image_side = SIDE // 2 if packed else SIDE
        which_half, in_cell = cell[:, None] // size, cell[:, None] % size
        pixel_half = places // image_side
        local_pos = places - pixel_half * image_side
        usable = ((which_half == 0) | (packed == 1)) & (level[:, None] >= 0)
        same_image = (pixel_half == which_half) & usable
        low_edge = in_cell * image_side // size
        high_edge = ((in_cell + 1) * image_side + size - 1) // size
        inside = same_image & (local_pos >= low_edge) & (local_pos < high_edge)
        numerator = local_pos * (size - 1)
        base_cell = numerator // (image_side - 1)
        fraction = (numerator - base_cell * (image_side - 1)).astype(np.float32) / np.float32(image_side - 1)
        weight = np.where(in_cell == base_cell, np.float32(1) - fraction, np.float32(0))
        weight = weight + np.where(in_cell == base_cell + 1, fraction, np.float32(0))
        weight = np.where(same_image, weight, np.float32(0)).astype(np.float32)
        pad = ((0, 0), (1, 1))
        pools.append(np.pad(inside.astype(np.float32), pad))
        ups.append(np.pad(weight, pad))
        valids.append(usable[:, 0].astype(np.float32))
    return np.stack(pools), np.stack(ups), np.stack(valids)


def swap_cores(x):
    return lax.ppermute(x, "row", [(0, 1), (1, 0)])


def from_partner(x, axis, step):
    count = lax.axis_size(axis)
    return lax.ppermute(x, axis, [(a, a ^ step) for a in range(count)])


def everyone(x, axis):
    return [x] + [from_partner(x, axis, s) for s in range(1, lax.axis_size(axis))]


def tree_sum(parts):
    while len(parts) > 1:
        parts = [parts[k] + parts[k + 1] for k in range(0, len(parts), 2)]
    return parts[0]


def sum_over(x, axis):
    return tree_sum(everyone(x, axis))


def scatter_blocks(block_of, axis):
    me = lax.axis_index(axis)
    return [block_of(me)] + [
        from_partner(block_of(me ^ s), axis, s) for s in range(1, lax.axis_size(axis))
    ]


def in_order(parts, axis):
    me = lax.axis_index(axis)
    out = jnp.zeros((len(parts),) + parts[0].shape, parts[0].dtype)
    for s, part in enumerate(parts):
        out = lax.dynamic_update_slice_in_dim(out, part[None], me ^ s, 0)
    return out


def img_grid():
    count = lax.axis_size("img")
    ny = 1 << (int(math.log2(count)) // 2)
    return ny, count // ny


def ring_step(x, axis):
    ny, nx = img_grid()
    if axis == "col":
        count = lax.axis_size("col")
        return lax.ppermute(x, "col", [(a, (a + 1) % count) for a in range(count)])
    pairs = []
    for a in range(ny):
        for b in range(nx):
            to = (a, (b + 1) % nx) if axis == "x" else ((a + 1) % ny, b)
            pairs.append((a * nx + b, to[0] * nx + to[1]))
    return lax.ppermute(x, "img", pairs)


def place_on(axis):
    ny, nx = img_grid()
    i = lax.axis_index("img")
    return {"col": lambda: (lax.axis_index("col"), lax.axis_size("col")), "y": lambda: (i // nx, ny), "x": lambda: (i % nx, nx)}[axis]()


def ring_gather(x, axis):
    _, count = place_on(axis)
    parts = [x]
    for _ in range(count - 1):
        parts.append(ring_step(parts[-1], axis))
    return parts


def ring_scatter(block_of, axis):
    _, count = place_on(axis)
    total = block_of(0)
    for t in range(1, count):
        total = (ring_step(total, axis).astype(F32) + block_of(t).astype(F32)).astype(BF16)
    return total


def per_device(
    canvases,
    layout,
    labels,
    branch_w,
    branch_gain,
    branch_bias,
    join_w,
    join_gain,
    join_bias,
    class_w,
    class_bias,
):
    canvas_count, height, width, channels = canvases.shape
    mid = join_w.shape[2]
    half_mid = mid // 2
    classes = class_w.shape[1]
    own_join = join_w.shape[0]
    own_branch = branch_w.shape[0]
    row, col, img = lax.axis_index("row"), lax.axis_index("col"), lax.axis_index("img")
    rows_n, cols_n, img_n = lax.axis_size("row"), lax.axis_size("col"), lax.axis_size("img")
    ny, nx = img_grid()
    tall = height * rows_n
    chip_pixels = canvas_count * tall * width
    total_pixels = chip_pixels * cols_n * img_n
    devices = cols_n * img_n
    group = row * cols_n + col
    group_c = channels // (rows_n * cols_n)
    col_c = channels // cols_n
    first = row == 0

    def own_half(x, axis=-1):
        return lax.dynamic_slice_in_dim(x, row * half_mid, half_mid, axis)

    def both_halves(x, axis=-1):
        other = swap_cores(x)
        return jnp.concatenate([jnp.where(first, x, other), jnp.where(first, other, x)], axis=axis)

    taps_first = jnp.transpose(join_w, (1, 0, 2))
    kept = own_half(taps_first)
    swapped = swap_cores(lax.dynamic_slice_in_dim(taps_first, (1 - row) * half_mid, half_mid, 2))
    main_w = jnp.where(first, kept, swapped)
    branch_part = jnp.where(first, swapped, kept)

    half_c = own_join // 2
    pieces = (main_w[:, :half_c], main_w[:, half_c:])
    group_weights = []
    current = list(pieces)
    for t in range(cols_n):
        got = []
        for piece, order in zip(current, (("x", "y"), ("y", "x"))):
            grid = [ring_gather(p, order[1]) for p in ring_gather(piece, order[0])]
            if order[0] == "x":
                grid = [[grid[b][a] for b in range(nx)] for a in range(ny)]
            got.append(grid)
        whole = jnp.zeros((TAPS, ny, nx, 2, half_c, half_mid), BF16)
        for half in range(2):
            for a in range(ny):
                for b in range(nx):
                    spot = ((img // nx - a) % ny, (img % nx - b) % nx)
                    whole = lax.dynamic_update_slice(
                        whole, got[half][a][b][:, None, None, None], (0, spot[0], spot[1], half, 0, 0)
                    )
        group_weights.append(whole.reshape(TAPS, col_c, half_mid))
        if t < cols_n - 1:
            current = [ring_step(p, "col") for p in current]

    block_m = half_mid // devices
    by_column = jnp.transpose(branch_part, (0, 2, 1)).reshape(TAPS, cols_n, img_n, block_m, own_join)
    by_column = jnp.transpose(by_column, (1, 2, 0, 3, 4))
    got_col = in_order(
        scatter_blocks(lambda d: lax.dynamic_index_in_dim(by_column, d, 0, keepdims=False), "col"), "col"
    )
    got_img = in_order(
        scatter_blocks(lambda d: lax.dynamic_index_in_dim(got_col, d, 1, keepdims=False), "img"), "img"
    )
    block_rows = TAPS * block_m
    branch_cols = jnp.transpose(got_img, (2, 3, 1, 0, 4)).reshape(block_rows, LEVELS * mid)

    zero_row = ((0, 0), (1, 1), (0, 0), (0, 0))
    ends = cols_n - 1
    left = lax.ppermute(canvases[:, :, -1], "col", [(a, a + 1) for a in range(ends)])
    right = lax.ppermute(canvases[:, :, 0], "col", [(a + 1, a) for a in range(ends)])
    other = swap_cores(canvases)
    sides = jnp.stack([left, right])
    other_sides = swap_cores(sides)

    def stacked(mine, theirs, axis):
        return jnp.concatenate([jnp.where(first, mine, theirs), jnp.where(first, theirs, mine)], axis=axis)

    full = stacked(canvases, other, 1)
    left, right = stacked(sides, other_sides, 2)
    views = [
        jnp.pad(v, zero_row)
        for v in (
            jnp.concatenate([left[:, :, None], full[:, :, :-1]], axis=2),
            full,
            jnp.concatenate([full[:, :, 1:], right[:, :, None]], axis=2),
        )
    ]

    slot_level, slot_a, slot_b, slot_second = slot_lists()
    slots = len(slot_level)
    pool_a, up_a, valid_a = (jnp.asarray(t) for t in axis_tables(slot_a, slot_level))
    pool_b, up_b, valid_b = (jnp.asarray(t) for t in axis_tables(slot_b, slot_level))
    may_pack = jnp.where(layout[0] == 1, 0, 1)
    second = jnp.asarray(slot_second)
    packed = jnp.where(second == 1, 0, layout[may_pack])
    slot_canvas = jnp.where(second == 1, 1 - may_pack, may_pack)

    def pick(table):
        return jnp.where((packed == 1).reshape((-1,) + (1,) * (table.ndim - 2)), table[1], table[0])

    pool_rows, pool_cols, up_rows, up_cols = pick(pool_a), pick(pool_b), pick(up_a), pick(up_b)
    mask = pick(valid_a) * pick(valid_b)
    counted = jnp.maximum(jnp.sum(pool_rows, 1) * jnp.sum(pool_cols, 1), 1.0)
    on_canvas = (slot_canvas[None, :] == jnp.arange(canvas_count)[:, None]).astype(F32)
    of_slot = jnp.asarray((slot_level[None, :] == np.arange(LEVELS)[:, None]).astype(np.float32))
    level_mask = of_slot * mask

    def pixel_table(rows, cols):
        table = rows.T[None, :, None, :] * cols.T[None, None, :, :]
        return (on_canvas[:, None, None, :] * table).astype(BF16)

    near_cols = lax.dynamic_slice_in_dim(up_cols, col * width, width + 2, 1)
    up_views = [pixel_table(up_rows, near_cols[:, dx : dx + width]) for dx in range(3)]
    pool_own = pixel_table(
        lax.dynamic_slice_in_dim(pool_rows, 1 + row * height, height, 1),
        lax.dynamic_slice_in_dim(pool_cols, 1 + col * width, width, 1),
    )

    pool_part = jnp.einsum("nyxq,nyxc->qc", pool_own, canvases, preferred_element_type=F32)
    half_channels = channels // rows_n
    mine = lax.dynamic_slice_in_dim(pool_part, row * half_channels, half_channels, 1)
    mine = mine + swap_cores(lax.dynamic_slice_in_dim(pool_part, (1 - row) * half_channels, half_channels, 1))
    pool_sums = tree_sum(
        scatter_blocks(lambda d: lax.dynamic_slice_in_dim(mine, d * group_c, group_c, 1), "col")
    )
    pooled = (pool_sums / counted[:, None]).astype(BF16)

    bw_rows = in_order(everyone(branch_w.reshape(own_branch, LEVELS * mid), "img"), "img")
    bw_rows = bw_rows.reshape(group_c, LEVELS * mid)

    def of_level(wide):
        k = wide.shape[1] // LEVELS
        return sum(of_slot[b][:, None] * wide[:, b * k : (b + 1) * k] for b in range(LEVELS))

    def to_levels(narrow):
        return jnp.concatenate([of_slot[b][:, None].astype(narrow.dtype) * narrow for b in range(LEVELS)], axis=1)

    def slot_rows(per_level):
        return sum(of_slot[b][:, None] * per_level[b][None] for b in range(LEVELS))

    def level_sums(per_slot):
        return jnp.stack([jnp.sum(level_mask[b][:, None] * per_slot, axis=0) for b in range(LEVELS)])

    pre_part = of_level(jnp.dot(pooled, bw_rows, preferred_element_type=F32))
    pre = own_half(pre_part) + swap_cores(lax.dynamic_slice_in_dim(pre_part, (1 - row) * half_mid, half_mid, 1))
    pre = sum_over(pre, "col")
    count_part = jnp.broadcast_to(jnp.sum(level_mask, 1)[:, None], (LEVELS, half_mid))
    stats = sum_over(jnp.concatenate([level_sums(pre), level_sums(pre * pre), count_part]), "img")
    counts = stats[2 * LEVELS :]
    bin_mean = stats[:LEVELS] / counts
    bin_rstd = lax.rsqrt(stats[LEVELS : 2 * LEVELS] / counts - bin_mean * bin_mean + epsilon)
    normed = (pre - slot_rows(bin_mean)) * slot_rows(bin_rstd)
    gain, bias = own_half(branch_gain), own_half(branch_bias)
    feature, gelu_back = jax.vjp(jax.nn.gelu, slot_rows(gain) * normed + slot_rows(bias))
    feature = (mask[:, None] * feature).astype(BF16)
    all_features = jnp.concatenate(everyone(feature, "img"), axis=0)
    all_features = both_halves(all_features)
    wide_features = jnp.concatenate(
        [to_levels(all_features[s * slots : (s + 1) * slots]) for s in range(img_n)], axis=0
    )

    cell_w = lax.dot_general(
        branch_cols, wide_features, (((1,), (1,)), ((), ())), preferred_element_type=F32
    ).astype(BF16)
    cell_w = [cell_w[:, s * slots : (s + 1) * slots] for s in range(img_n)]
    cell_w = in_order([cell_w[0]] + [from_partner(cell_w[s], "img", s) for s in range(1, img_n)], "img")
    cell_w = in_order(everyone(cell_w, "col"), "col")
    cell_w = cell_w.reshape(devices, TAPS, block_m, slots)
    cell_w = jnp.transpose(cell_w, (1, 0, 2, 3)).reshape(TAPS, half_mid, slots)

    joined = jnp.zeros((chip_pixels, half_mid), F32)
    for t in range(cols_n):
        source = (col - t) % cols_n
        for k in range(TAPS):
            view = views[k % 3][:, k // 3 : k // 3 + tall]
            view = lax.dynamic_slice_in_dim(view, source * col_c, col_c, 3).reshape(chip_pixels, col_c)
            joined = joined + jnp.dot(view, group_weights[t][k], preferred_element_type=F32)
    for k in range(TAPS):
        view = up_views[k % 3][:, k // 3 : k // 3 + tall].reshape(chip_pixels, slots)
        joined = joined + lax.dot_general(
            view, cell_w[k], (((1,), (1,)), ((), ())), preferred_element_type=F32
        )

    def sum_chips(x):
        return sum_over(sum_over(x, "img"), "col")

    head_sum = sum_chips(jnp.stack([jnp.sum(joined, 0), jnp.sum(joined * joined, 0)]))
    head_mean = head_sum[0] / total_pixels
    head_rstd = lax.rsqrt(head_sum[1] / total_pixels - head_mean * head_mean + epsilon)
    normed_head = (joined - head_mean) * head_rstd
    head_gain, head_bias = own_half(join_gain), own_half(join_bias)
    activated, head_gelu_back = jax.vjp(jax.nn.gelu, head_gain * normed_head + head_bias)
    act_low = activated.astype(BF16)
    own_class_w = own_half(class_w, 0)
    logits_part = lax.dot_general(
        own_class_w, act_low, (((0,), (1,)), ((), ())), preferred_element_type=F32
    )
    logits = logits_part + swap_cores(logits_part) + class_bias[:, None]
    row_peak = jnp.max(logits, axis=0, keepdims=True)
    exp_terms = jnp.exp(logits - row_peak)
    probabilities = exp_terms / jnp.sum(exp_terms, axis=0, keepdims=True)
    chip_labels = stacked(labels, swap_cores(labels), 1).reshape(1, chip_pixels)
    onehot = (chip_labels == jnp.arange(classes, dtype=jnp.int32)[:, None]).astype(F32)
    dlogits = ((probabilities - onehot) / math.sqrt(total_pixels)).astype(BF16)
    class_part = jnp.dot(dlogits, act_low, preferred_element_type=F32)
    class_bias_part = jnp.sum(dlogits.astype(F32), axis=1)
    grad_act = lax.dot_general(
        dlogits, own_class_w, (((0,), (1,)), ((), ())), preferred_element_type=F32
    )
    grad_head = head_gelu_back(grad_act)[0]
    head_parts = jnp.concatenate(
        [
            jnp.sum(grad_head, 0)[None],
            jnp.sum(grad_head * normed_head, 0)[None],
            class_part,
            jnp.pad(class_bias_part, (0, half_mid - classes))[None],
        ]
    )
    head_totals = sum_chips(head_parts)
    grad_joined = (
        head_gain * head_rstd * (grad_head - (head_totals[0] + normed_head * head_totals[1]) / total_pixels)
    ).astype(BF16).reshape(canvas_count, tall, width, half_mid)
    head_all = both_halves(head_totals)
    grad_join_bias, grad_join_gain = head_all[0], head_all[1]
    grad_class_w = head_all[2 : 2 + classes].T
    grad_class_bias = head_totals[2 + classes, :classes]

    g_left = lax.ppermute(grad_joined[:, :, -1], "col", [(a, a + 1) for a in range(ends)])
    g_right = lax.ppermute(grad_joined[:, :, 0], "col", [(a + 1, a) for a in range(ends)])
    shifted = [
        jnp.pad(v, zero_row)
        for v in (
            jnp.concatenate([g_left[:, :, None], grad_joined[:, :, :-1]], axis=2),
            grad_joined,
            jnp.concatenate([grad_joined[:, :, 1:], g_right[:, :, None]], axis=2),
        )
    ]
    grad_views = jnp.concatenate(
        [shifted[2 - k % 3][:, 2 - k // 3 : 2 - k // 3 + tall] for k in range(TAPS)], axis=3
    ).reshape(chip_pixels, TAPS * half_mid)

    flat = full.reshape(chip_pixels, channels)

    def chunk_of(t):
        dest = (col - 1 - t) % cols_n
        chunk = lax.dynamic_slice_in_dim(flat, dest * col_c, col_c, 1)
        part = lax.dot_general(
            chunk, grad_views, (((0,), (0,)), ((), ())), preferred_element_type=F32
        ).astype(BF16)
        part = part.reshape(ny, nx, 2, half_c, TAPS * half_mid)
        done = []
        for half in range(2):
            this = part[:, :, half]
            order = ("x", "y") if half == 0 else ("y", "x")
            dims = {"x": 1, "y": 0}
            place, count = place_on(order[0])
            other = 1 - dims[order[0]]

            def first_block(s, this=this, order=order, place=place, count=count):
                return lax.dynamic_index_in_dim(this, (place - 1 - s) % count, dims[order[0]], keepdims=False)

            line = ring_scatter(first_block, order[0])
            place2, count2 = place_on(order[1])

            def second_block(s, line=line, place2=place2, count2=count2):
                return lax.dynamic_index_in_dim(line, (place2 - 1 - s) % count2, 0, keepdims=False)

            done.append(ring_scatter(second_block, order[1]))
        return done

    chunks = [chunk_of(t) for t in range(cols_n)]
    main_grad = jnp.concatenate(
        [ring_scatter(lambda t, half=half: chunks[t][half], "col") for half in range(2)], axis=0
    ).reshape(own_join, TAPS, half_mid)

    up_flat = up_views[1][:, 1 : 1 + tall].reshape(chip_pixels, slots)
    cell_grad = lax.dot_general(
        grad_views, up_flat, (((0,), (0,)), ((), ())), preferred_element_type=F32
    ).astype(BF16)
    cell_grad = jnp.transpose(cell_grad.reshape(TAPS, cols_n, img_n, block_m, slots), (1, 2, 0, 3, 4))
    cell_grad = tree_sum(
        [
            p.astype(F32)
            for p in scatter_blocks(lambda d: lax.dynamic_index_in_dim(cell_grad, d, 0, keepdims=False), "col")
        ]
    ).astype(BF16)
    cell_grad = scatter_blocks(lambda d: lax.dynamic_index_in_dim(cell_grad, d, 0, keepdims=False), "img")
    cell_grad = jnp.concatenate([c.reshape(block_rows, slots) for c in cell_grad], axis=1)

    branch_grad = jnp.dot(cell_grad, wide_features, preferred_element_type=F32).astype(BF16)
    branch_grad = jnp.transpose(branch_grad.reshape(block_rows, cols_n, img_n, own_join), (1, 2, 0, 3))
    branch_grad = in_order(
        scatter_blocks(lambda d: lax.dynamic_index_in_dim(branch_grad, d, 0, keepdims=False), "col"), "col"
    )
    branch_grad = in_order(
        scatter_blocks(lambda d: lax.dynamic_index_in_dim(branch_grad, d, 1, keepdims=False), "img"), "img"
    )
    branch_grad = branch_grad.reshape(img_n, cols_n, TAPS, block_m, own_join)
    branch_grad = jnp.transpose(branch_grad, (4, 2, 1, 0, 3)).reshape(own_join, TAPS, half_mid)

    sent = swap_cores(jnp.where(first, branch_grad, main_grad))
    kept = jnp.where(first, main_grad, branch_grad)
    grad_join_w = jnp.concatenate([jnp.where(first, kept, sent), jnp.where(first, sent, kept)], axis=2).astype(F32)

    feature_grad = jnp.concatenate(
        [
            of_level(
                lax.dot_general(
                    cell_grad[:, s * slots : (s + 1) * slots],
                    branch_cols,
                    (((0,), (0,)), ((), ())),
                    preferred_element_type=F32,
                )
            )
            for s in range(img_n)
        ],
        axis=0,
    )
    feature_grad = own_half(feature_grad) + swap_cores(
        lax.dynamic_slice_in_dim(feature_grad, (1 - row) * half_mid, half_mid, 1).astype(BF16)
    ).astype(F32)
    parts = [feature_grad[s * slots : (s + 1) * slots].astype(BF16) for s in range(img_n)]
    parts = [parts[0]] + [from_partner(parts[s], "img", s) for s in range(1, img_n)]
    feature_grad = tree_sum([p.astype(F32) for p in parts]).astype(BF16)
    feature_grad = tree_sum([p.astype(F32) for p in everyone(feature_grad, "col")])

    grad_y = gelu_back(feature_grad)[0]
    bin_totals = sum_over(jnp.concatenate([level_sums(grad_y), level_sums(grad_y * normed)]), "img")
    correction = mask[:, None] * (
        slot_rows(bin_totals[:LEVELS] / counts) + normed * slot_rows(bin_totals[LEVELS:] / counts)
    )
    grad_pre = (slot_rows(gain) * slot_rows(bin_rstd) * (grad_y - correction)).astype(BF16)
    grad_pre = to_levels(both_halves(grad_pre))
    bin_totals = both_halves(bin_totals)
    grad_branch_bias, grad_branch_gain = bin_totals[:LEVELS], bin_totals[LEVELS:]

    weight_grad = lax.dot_general(
        pooled, grad_pre, (((0,), (0,)), ((), ())), preferred_element_type=F32
    ).astype(BF16)
    grad_branch_w = tree_sum(
        [
            p.astype(F32)
            for p in scatter_blocks(
                lambda d: lax.dynamic_slice_in_dim(weight_grad, d * own_branch, own_branch, 0), "img"
            )
        ]
    ).reshape(own_branch, LEVELS, mid)

    grad_pooled = lax.dot_general(grad_pre, bw_rows, (((1,), (1,)), ((), ())), preferred_element_type=F32)
    grad_pooled = (grad_pooled / counted[:, None]).astype(BF16)
    grad_pooled = in_order(everyone(grad_pooled, "col"), "col")
    grad_pooled = jnp.transpose(grad_pooled, (1, 0, 2)).reshape(slots, half_channels)
    grad_pooled = both_halves(grad_pooled)

    grad_groups = [None] * cols_n
    grad_cat = jnp.zeros((chip_pixels, channels), F32)
    for t in range(cols_n):
        source = (col - t) % cols_n
        weight = jnp.transpose(group_weights[t], (0, 2, 1)).reshape(TAPS * half_mid, col_c)
        part = jnp.dot(grad_views, weight, preferred_element_type=F32)
        grad_cat = lax.dynamic_update_slice_in_dim(grad_cat, part, source * col_c, 1)
    grad_cat = grad_cat.reshape(canvas_count, tall, width, channels)
    mine = lax.dynamic_slice_in_dim(grad_cat, row * height, height, 1)
    theirs = lax.dynamic_slice_in_dim(grad_cat, (1 - row) * height, height, 1).astype(BF16)
    pool_back = jnp.einsum("nyxq,qc->nyxc", pool_own, grad_pooled, preferred_element_type=F32)
    grad_canvases = mine + swap_cores(theirs).astype(F32) + pool_back

    logits = lax.dynamic_slice_in_dim(
        logits.T.reshape(canvas_count, tall, width, classes), row * height, height, 1
    )
    return (
        logits,
        grad_canvases,
        grad_branch_w,
        grad_branch_gain,
        grad_branch_bias,
        grad_join_w,
        grad_join_gain,
        grad_join_bias,
        grad_class_w,
        grad_class_bias,
    )


def solution(mesh):
    in_specs = (
        P("img", "row", "col", None),
        P("img"),
        P("img", "row", "col"),
        P(("row", "col", "img"), None, None),
        P(),
        P(),
        P(("row", "col", "img"), None, None),
        P(),
        P(),
        P(),
        P(),
    )
    out_specs = (
        P("img", "row", "col", None),
        P("img", "row", "col", None),
        P(("row", "col", "img"), None, None),
        P(),
        P(),
        P(("row", "col", "img"), None, None),
        P(),
        P(),
        P(),
        P(),
    )
    return jax.shard_map(
        per_device, mesh=mesh, in_specs=in_specs, out_specs=out_specs, check_vma=False
    )
```

```python
import functools
import math

import jax
import jax.numpy as jnp
import numpy as np
from jax import lax
from jax.experimental import pallas as pl
from jax.experimental.pallas import tpu as pltpu
from jax.sharding import PartitionSpec as P

SIDE = 64
bin_scales = (1, 2, 3, 6)
epsilon = 1e-05
LEVELS = len(bin_scales)
TAPS = 9
BF16 = jnp.bfloat16
F32 = jnp.float32


def slot_lists():
    rows = []
    for level, size in enumerate(bin_scales):
        rows += [(level, a, b, 0) for a in range(2 * size) for b in range(2 * size)]
    for level, size in enumerate(bin_scales):
        rows += [(level, a, b, 1) for a in range(size) for b in range(size)]
    rows += [(-1, 0, 0, 1)] * (-len(rows) % 128)
    return [np.array(column) for column in zip(*rows)]


def axis_tables(cell, level):
    size = np.array(bin_scales)[np.maximum(level, 0)][:, None]
    places = np.arange(SIDE)[None, :]
    pools, ups, valids = [], [], []
    for packed in (0, 1):
        image_side = SIDE // 2 if packed else SIDE
        which_half, in_cell = cell[:, None] // size, cell[:, None] % size
        pixel_half = places // image_side
        local_pos = places - pixel_half * image_side
        usable = ((which_half == 0) | (packed == 1)) & (level[:, None] >= 0)
        same_image = (pixel_half == which_half) & usable
        low_edge = in_cell * image_side // size
        high_edge = ((in_cell + 1) * image_side + size - 1) // size
        inside = same_image & (local_pos >= low_edge) & (local_pos < high_edge)
        numerator = local_pos * (size - 1)
        base_cell = numerator // (image_side - 1)
        fraction = (numerator - base_cell * (image_side - 1)).astype(np.float32) / np.float32(image_side - 1)
        weight = np.where(in_cell == base_cell, np.float32(1) - fraction, np.float32(0))
        weight = weight + np.where(in_cell == base_cell + 1, fraction, np.float32(0))
        weight = np.where(same_image, weight, np.float32(0)).astype(np.float32)
        pad = ((0, 0), (1, 1))
        pools.append(np.pad(inside.astype(np.float32), pad))
        ups.append(np.pad(weight, pad))
        valids.append(usable[:, 0].astype(np.float32))
    return np.stack(pools), np.stack(ups), np.stack(valids)


def swap_cores(x):
    return lax.ppermute(x, "row", [(0, 1), (1, 0)])


def exchange(blocks, axis):
    return lax.all_to_all(blocks, axis, 0, 0, tiled=True)


def everyone(x, axis):
    return exchange(jnp.broadcast_to(x[None], (lax.axis_size(axis),) + x.shape), axis)


def sum_over(x, axis):
    return jnp.sum(everyone(x, axis).astype(F32), axis=0)


def img_grid():
    count = lax.axis_size("img")
    ny = 1 << (int(math.log2(count)) // 2)
    return ny, count // ny


def ring_step(x, axis):
    ny, nx = img_grid()
    if axis == "col":
        count = lax.axis_size("col")
        return lax.ppermute(x, "col", [(a, (a + 1) % count) for a in range(count)])
    pairs = []
    for a in range(ny):
        for b in range(nx):
            to = (a, (b + 1) % nx) if axis == "x" else ((a + 1) % ny, b)
            pairs.append((a * nx + b, to[0] * nx + to[1]))
    return lax.ppermute(x, "img", pairs)


def place_on(axis):
    ny, nx = img_grid()
    i = lax.axis_index("img")
    return {"col": lambda: (lax.axis_index("col"), lax.axis_size("col")), "y": lambda: (i // nx, ny), "x": lambda: (i % nx, nx)}[axis]()


def ring_gather(x, axis):
    _, count = place_on(axis)
    parts = [x]
    for _ in range(count - 1):
        parts.append(ring_step(parts[-1], axis))
    return parts


def ring_scatter(block_of, axis):
    _, count = place_on(axis)
    total = block_of(0)
    for t in range(1, count):
        total = (ring_step(total, axis).astype(F32) + block_of(t).astype(F32)).astype(BF16)
    return total


VMEM_LIMIT = 56 << 20


def cost(microseconds):
    return pl.CostEstimate(
        flops=int(microseconds * 1.1e9), bytes_accessed=int(microseconds * 3.6e6), transcendentals=0
    )


def shifted(block, column, step, width):
    rows = block.shape[0]
    edge = jnp.broadcast_to(column[:, None, :], (rows // width, width, column.shape[-1])).reshape(block.shape)
    x = lax.broadcasted_iota(jnp.int32, block.shape, 0) % width
    moved = pltpu.roll(block, step % rows, 0)
    return jnp.where(x == (0 if step == 1 else width - 1), edge, moved)


def join_kernel(me, *refs, height, width, grid, has_acc, extra):
    mine, theirs = refs[:3], refs[3:6]
    pieces = (refs[6:8], refs[8:10])
    acc_ref = refs[10] if has_acc else None
    out_ref, w_ref, token_ref, rows_ref = refs[10 + has_acc + extra :]
    lanes = mine[0].shape[-1]
    tall = 2 * height
    half_c = pieces[0][0].shape[2]

    @pl.when(pl.program_id(0) == 0)
    def _():
        token_ref[...] = jnp.zeros(token_ref.shape, F32)
        rows_ref[:width] = jnp.zeros((width, 3 * lanes), BF16)
        rows_ref[(tall + 1) * width :] = jnp.zeros((width, 3 * lanes), BF16)
        for half in range(2):
            for second, ref in enumerate(pieces[half]):
                for one in range(ref.shape[0]):
                    back_y, back_x = (second, one) if half == 0 else (one, second)
                    spot_y = (me[2] + grid[0] - back_y) % grid[0]
                    spot_x = (me[3] + grid[1] - back_x) % grid[1]
                    start = pl.multiple_of(((spot_y * grid[1] + spot_x) * 2 + half) * half_c, half_c)
                    w_ref[:, pl.ds(start, half_c), :] = ref[one]

    band = 16
    for part, (x_ref, left_ref, right_ref) in enumerate((mine, theirs)):
        first_row = (me[0] if part == 0 else 1 - me[0]) * height

        def fill(i, _, x_ref=x_ref, left_ref=left_ref, right_ref=right_ref, first_row=first_row):
            ys = pl.ds(pl.multiple_of(i * band, band), band)
            to = pl.ds(pl.multiple_of((first_row + 1 + i * band) * width, width), band * width)
            for lane in range(0, lanes, 128):
                at = slice(lane, lane + 128)
                x = x_ref[0, ys, :, at].reshape(band * width, 128)
                wide = x.astype(F32)
                before = shifted(wide, left_ref[0, ys, at].astype(F32), 1, width)
                after = shifted(wide, right_ref[0, ys, at].astype(F32), -1, width)
                rows_ref[to, lane : lane + 128] = before.astype(BF16)
                rows_ref[to, lanes + lane : lanes + lane + 128] = x
                rows_ref[to, 2 * lanes + lane : 2 * lanes + lane + 128] = after.astype(BF16)
            return 0

        lax.fori_loop(0, height // band, fill, 0)
    total = acc_ref[0] if has_acc else jnp.zeros(out_ref.shape[1:], F32)
    for dy in range(3):
        total = total + jnp.dot(
            rows_ref[dy * width : (dy + tall) * width],
            w_ref[3 * dy : 3 * dy + 3].reshape(3 * lanes, -1),
            preferred_element_type=F32,
        )
    out_ref[0] = total


ANYWHERE = pl.BlockSpec(memory_space=pl.ANY)


def join_group(me, back, groups, mine, theirs, pieces, acc, grid, ahead):
    count, height, width, _ = mine[0].shape
    tall = 2 * height
    taps, m = pieces[0].shape[1], pieces[0].shape[3]
    lanes = sum(p.shape[0] * p.shape[2] for p in pieces)
    image = pl.BlockSpec((1, height, width, lanes), lambda n, p: (n, 0, 0, (p[1] + groups - back) % groups))
    edge = pl.BlockSpec((1, height, lanes), lambda n, p: (n, 0, (p[1] + groups - back) % groups))
    spec = pltpu.PrefetchScalarGridSpec(
        num_scalar_prefetch=1,
        grid=(count,),
        in_specs=[image, edge, edge] * 2
        + [pl.BlockSpec(p.shape, lambda n, p: (0, 0, 0, 0)) for p in pieces]
        + [pl.BlockSpec((1, tall * width, m), lambda n, p: (n, 0, 0))] * (acc is not None)
        + [ANYWHERE] * len(ahead),
        out_specs=[
            pl.BlockSpec((1, tall * width, m), lambda n, p: (n, 0, 0)),
            pl.BlockSpec((taps, lanes, m), lambda n, p: (0, 0, 0)),
            pl.BlockSpec((8, 128), lambda n, p: (0, 0)),
        ],
        scratch_shapes=[pltpu.VMEM(((tall + 2) * width, 3 * lanes), BF16)],
    )
    return pl.pallas_call(
        functools.partial(join_kernel, height=height, width=width, grid=grid, has_acc=acc is not None, extra=len(ahead)),
        grid_spec=spec,
        out_shape=[
            jax.ShapeDtypeStruct((count, tall * width, m), F32),
            jax.ShapeDtypeStruct((taps, lanes, m), BF16),
            jax.ShapeDtypeStruct((8, 128), F32),
        ],
        input_output_aliases={11: 0} if acc is not None else {},
        compiler_params=pltpu.CompilerParams(vmem_limit_bytes=VMEM_LIMIT),
        cost_estimate=cost(11),
        name="join_group",
    )(me, *mine, *theirs, *pieces, *([] if acc is None else [acc]), *ahead)


def cell_weights_kernel(me, cols_ref, level_ref, mine_ref, theirs_ref, token_ref, out_ref):
    imgs, slots, half = mine_ref.shape
    rows = cols_ref.shape[0]
    for s in range(imgs):
        total = jnp.zeros((rows, slots), F32)
        for b in range(LEVELS):
            part = jnp.zeros((rows, slots), F32)
            for ref, side in ((mine_ref, me[0]), (theirs_ref, 1 - me[0])):
                at = pl.ds(pl.multiple_of(2 * b * half + side * half, half), half)
                part = part + lax.dot_general(
                    cols_ref[:, at], ref[s], (((1,), (1,)), ((), ())), preferred_element_type=F32
                )
            total = total + level_ref[b : b + 1, :] * part
        out_ref[s] = total.astype(BF16)


def cell_weights(me, cols, of_slot, mine, theirs, token):
    whole = lambda a: pl.BlockSpec(a.shape, lambda i, p, r=a.ndim: (0,) * r)
    out = jax.ShapeDtypeStruct((mine.shape[0], cols.shape[0], mine.shape[1]), BF16)
    return pl.pallas_call(
        cell_weights_kernel,
        grid_spec=pltpu.PrefetchScalarGridSpec(
            num_scalar_prefetch=1,
            grid=(1,),
            in_specs=[whole(cols), whole(of_slot), whole(mine), whole(theirs), ANYWHERE],
            out_specs=whole(out),
        ),
        out_shape=out,
        compiler_params=pltpu.CompilerParams(vmem_limit_bytes=VMEM_LIMIT),
        cost_estimate=cost(4),
        name="cell_weights",
    )(me, cols, of_slot, mine, theirs, token)


def cell_back_kernel(me, cols_ref, level_ref, mine_ref, theirs_ref, grad_ref, branch_ref, own_ref, send_ref):
    imgs, slots, half = mine_ref.shape
    rows = cols_ref.shape[0]
    for b in range(LEVELS):
        level = level_ref[b : b + 1, :].astype(BF16)
        for ref, side in ((mine_ref, me[0]), (theirs_ref, 1 - me[0])):
            total = jnp.zeros((rows, half), F32)
            for s in range(imgs):
                total = total + jnp.dot(grad_ref[s] * level, ref[s], preferred_element_type=F32)
            branch_ref[:, pl.ds(pl.multiple_of(2 * b * half + side * half, half), half)] = total.astype(BF16)
    for s in range(imgs):
        for ref, side in ((own_ref, me[0]), (send_ref, 1 - me[0])):
            total = jnp.zeros((slots, half), F32)
            for b in range(LEVELS):
                at = pl.ds(pl.multiple_of(2 * b * half + side * half, half), half)
                level = level_ref[b : b + 1, :].astype(BF16)
                total = total + lax.dot_general(
                    grad_ref[s] * level, cols_ref[:, at], (((0,), (0,)), ((), ())), preferred_element_type=F32
                )
            ref[s] = total.astype(ref.dtype)


def cell_back(me, cols, of_slot, mine, theirs, grad):
    whole = lambda a: pl.BlockSpec(a.shape, lambda i, p, r=a.ndim: (0,) * r)
    outs = [
        jax.ShapeDtypeStruct(cols.shape, BF16),
        jax.ShapeDtypeStruct(mine.shape, F32),
        jax.ShapeDtypeStruct(mine.shape, BF16),
    ]
    return pl.pallas_call(
        cell_back_kernel,
        grid_spec=pltpu.PrefetchScalarGridSpec(
            num_scalar_prefetch=1,
            grid=(1,),
            in_specs=[whole(a) for a in (cols, of_slot, mine, theirs, grad)],
            out_specs=[whole(a) for a in outs],
        ),
        out_shape=outs,
        compiler_params=pltpu.CompilerParams(vmem_limit_bytes=VMEM_LIMIT),
        cost_estimate=cost(5),
        name="cell_back",
    )(me, cols, of_slot, mine, theirs, grad)


def cells_kernel(up_ref, w_ref, acc_ref, out_ref, sums_ref, *, tall, width):
    slots = w_ref.shape[2]
    total = acc_ref[0]
    for k in range(TAPS):
        dy, dx = k // 3, k % 3
        total = total + lax.dot_general(
            up_ref[0, dy * width : (dy + tall) * width, dx * slots : (dx + 1) * slots],
            w_ref[k],
            (((1,), (1,)), ((), ())),
            preferred_element_type=F32,
        )
    out_ref[0] = total
    sums = jnp.concatenate([jnp.sum(total, 0, keepdims=True), jnp.sum(total * total, 0, keepdims=True)])

    @pl.when(pl.program_id(0) == 0)
    def _():
        sums_ref[...] = sums

    @pl.when(pl.program_id(0) > 0)
    def _():
        sums_ref[...] += sums


def join_cells(up, cell_w, acc, width):
    count, pixels, m = acc.shape
    rows = up.shape[1]
    return pl.pallas_call(
        functools.partial(cells_kernel, tall=pixels // width, width=width),
        grid=(count,),
        in_specs=[
            pl.BlockSpec((1, rows, up.shape[2]), lambda n: (n, 0, 0)),
            pl.BlockSpec(cell_w.shape, lambda n: (0, 0, 0)),
            pl.BlockSpec((1, pixels, m), lambda n: (n, 0, 0)),
        ],
        out_specs=[
            pl.BlockSpec((1, pixels, m), lambda n: (n, 0, 0)),
            pl.BlockSpec((2, m), lambda n: (0, 0)),
        ],
        out_shape=[jax.ShapeDtypeStruct(acc.shape, F32), jax.ShapeDtypeStruct((2, m), F32)],
        input_output_aliases={2: 0},
        compiler_params=pltpu.CompilerParams(vmem_limit_bytes=VMEM_LIMIT),
        cost_estimate=cost(6),
        name="join_cells",
    )(up, cell_w, acc)


def views_kernel(me, g_ref, left_ref, right_ref, out_ref, rows_ref, *, tall, width):
    m = g_ref.shape[-1]
    rows_ref[:, :width] = jnp.zeros((3, width, m), BF16)
    rows_ref[:, (tall + 1) * width :] = jnp.zeros((3, width, m), BF16)
    g = g_ref[0].astype(F32)
    inner = slice(width, (tall + 1) * width)
    rows_ref[0, inner] = shifted(g, left_ref[0].astype(F32), 1, width).astype(BF16)
    rows_ref[1, inner] = g_ref[0]
    rows_ref[2, inner] = shifted(g, right_ref[0].astype(F32), -1, width).astype(BF16)
    part_pixels = tall * width // 2
    for part in range(2):
        for k in range(TAPS):
            dy, dx = 2 - k // 3, 2 - k % 3
            start = dy * width + (me[0] if part == 0 else 1 - me[0]) * part_pixels
            out_ref[part, 0, :, k * m : (k + 1) * m] = rows_ref[
                dx, pl.ds(pl.multiple_of(start, width), part_pixels)
            ]


def gradient_views(me, g, left, right, width):
    count, pixels, m = g.shape
    tall = pixels // width
    return pl.pallas_call(
        functools.partial(views_kernel, tall=tall, width=width),
        grid_spec=pltpu.PrefetchScalarGridSpec(
            num_scalar_prefetch=1,
            grid=(count,),
            in_specs=[
                pl.BlockSpec((1, pixels, m), lambda n, p: (n, 0, 0)),
                pl.BlockSpec((1, tall, m), lambda n, p: (n, 0, 0)),
                pl.BlockSpec((1, tall, m), lambda n, p: (n, 0, 0)),
            ],
            out_specs=pl.BlockSpec((2, 1, pixels // 2, TAPS * m), lambda n, p: (0, n, 0, 0)),
            scratch_shapes=[pltpu.VMEM((3, (tall + 2) * width, m), BF16)],
        ),
        out_shape=jax.ShapeDtypeStruct((2, count, pixels // 2, TAPS * m), BF16),
        compiler_params=pltpu.CompilerParams(vmem_limit_bytes=VMEM_LIMIT),
        cost_estimate=cost(6),
        name="gradient_views",
    )(me, g, left, right)


def back_kernel(me, *refs, extra):
    g_ref, w_ref = refs[:2]
    theirs_ref, mine_ref, token_ref = refs[2 + extra :]
    taps, lanes, m = w_ref.shape
    total = jnp.zeros((g_ref.shape[2], lanes), F32)
    for k in range(taps):
        total = total + lax.dot_general(
            g_ref[0, 0, :, k * m : (k + 1) * m], w_ref[k], (((1,), (1,)), ((), ())), preferred_element_type=F32
        )

    @pl.when(pl.program_id(0) == 0)
    def _():
        theirs_ref[0] = total.astype(BF16)
        token_ref[...] = jnp.zeros(token_ref.shape, F32)

    @pl.when(pl.program_id(0) == 1)
    def _():
        mine_ref[0] = total


def back_group(me, back, groups, views, weights, mine, channels, ahead):
    _, count, pixels, _ = views.shape
    taps, lanes, m = weights.shape
    ahead = ([] if mine is None else [mine]) + ahead
    spec = pltpu.PrefetchScalarGridSpec(
        num_scalar_prefetch=1,
        grid=(2, count),
        in_specs=[
            pl.BlockSpec((1, 1, pixels, taps * m), lambda h, n, p: (1 - h, n, 0, 0)),
            pl.BlockSpec((taps, lanes, m), lambda h, n, p: (0, 0, 0)),
        ]
        + [ANYWHERE] * len(ahead),
        out_specs=[
            pl.BlockSpec((1, pixels, lanes), lambda h, n, p: (jnp.where(h == 0, n, count - 1), 0, 0)),
            pl.BlockSpec((1, pixels, lanes), lambda h, n, p: (jnp.where(h == 1, n, 0), 0, (p[1] + groups - back) % groups)),
            pl.BlockSpec((8, 128), lambda h, n, p: (0, 0)),
        ],
    )
    return pl.pallas_call(
        functools.partial(back_kernel, extra=len(ahead)),
        grid_spec=spec,
        out_shape=[
            jax.ShapeDtypeStruct((count, pixels, lanes), BF16),
            jax.ShapeDtypeStruct((count, pixels, channels), F32),
            jax.ShapeDtypeStruct((8, 128), F32),
        ],
        input_output_aliases={} if mine is None else {3: 1},
        compiler_params=pltpu.CompilerParams(vmem_limit_bytes=VMEM_LIMIT),
        cost_estimate=cost(10),
        name="canvas_gradient",
    )(me, views, weights, *ahead)


def finish_kernel(me, pool_ref, cells_ref, mine_ref, *refs):
    theirs, out_ref = refs[:-1], refs[-1]
    total = mine_ref[0] + jnp.dot(pool_ref[0], cells_ref[...], preferred_element_type=F32)
    for t, ref in enumerate(theirs):

        @pl.when(pl.program_id(0) == t)
        def _(ref=ref):
            out_ref[0] = total + ref[0].astype(F32)


def finish_canvases(me, pool, cells, mine, theirs):
    count, pixels, channels = mine.shape
    groups = len(theirs)
    lanes = channels // groups
    slots = cells.shape[0]

    def lane_block(t, p):
        return (p[1] - t + groups) % groups

    return pl.pallas_call(
        finish_kernel,
        grid_spec=pltpu.PrefetchScalarGridSpec(
            num_scalar_prefetch=1,
            grid=(groups, count),
            in_specs=[
                pl.BlockSpec((1, pixels, slots), lambda t, n, p: (n, 0, 0)),
                pl.BlockSpec((slots, lanes), lambda t, n, p: (0, lane_block(t, p))),
                pl.BlockSpec((1, pixels, lanes), lambda t, n, p: (n, 0, lane_block(t, p))),
            ]
            + [
                pl.BlockSpec(
                    (1, pixels, lanes), lambda t, n, p, s=s: (jnp.where(t == s, n, jnp.where(t < s, 0, count - 1)), 0, 0)
                )
                for s in range(groups)
            ],
            out_specs=pl.BlockSpec((1, pixels, lanes), lambda t, n, p: (n, 0, lane_block(t, p))),
        ),
        out_shape=jax.ShapeDtypeStruct(mine.shape, F32),
        compiler_params=pltpu.CompilerParams(vmem_limit_bytes=VMEM_LIMIT),
        cost_estimate=cost(11),
        name="finish_canvases",
    )(me, pool, cells, mine, *theirs)


def per_device(
    canvases,
    layout,
    labels,
    branch_w,
    branch_gain,
    branch_bias,
    join_w,
    join_gain,
    join_bias,
    class_w,
    class_bias,
):
    canvas_count, height, width, channels = canvases.shape
    mid = join_w.shape[2]
    half_mid = mid // 2
    classes = class_w.shape[1]
    own_join = join_w.shape[0]
    own_branch = branch_w.shape[0]
    row, col, img = lax.axis_index("row"), lax.axis_index("col"), lax.axis_index("img")
    rows_n, cols_n, img_n = lax.axis_size("row"), lax.axis_size("col"), lax.axis_size("img")
    ny, nx = img_grid()
    tall = height * rows_n
    chip_pixels = canvas_count * tall * width
    total_pixels = chip_pixels * cols_n * img_n
    devices = cols_n * img_n
    group = row * cols_n + col
    group_c = channels // (rows_n * cols_n)
    col_c = channels // cols_n
    first = row == 0
    use_kernels = width % 16 == 0 and height % 16 == 0 and own_join % 32 == 0 and nx == ny == 2

    def own_half(x, axis=-1):
        return lax.dynamic_slice_in_dim(x, row * half_mid, half_mid, axis)

    def both_halves(x, axis=-1):
        other = swap_cores(x)
        return jnp.concatenate([jnp.where(first, x, other), jnp.where(first, other, x)], axis=axis)

    taps_first = jnp.transpose(join_w, (1, 0, 2))
    kept = own_half(taps_first)
    swapped = swap_cores(lax.dynamic_slice_in_dim(taps_first, (1 - row) * half_mid, half_mid, 2))
    main_w = jnp.where(first, kept, swapped)
    branch_part = jnp.where(first, swapped, kept)

    me = jnp.stack([row, col, img // nx, img % nx]).astype(jnp.int32)

    def after(x, token):
        return x + token[0, 0].astype(x.dtype)

    def behind(x, other):
        return x + (other[(0,) * other.ndim] * 0).astype(x.dtype)

    half_c = own_join // 2
    place_y, place_x = img // nx, img % nx
    shards, first_rings, group_pieces, tokens = [main_w], [], [], []

    def gather_shard(t):
        if len(shards) <= t < cols_n:
            last = shards[-1] if t < 3 else after(shards[-1], tokens[t - 3])
            shards.append(ring_step(last, "col"))

    def gather_first(t):
        if len(first_rings) <= t < cols_n:
            stacks = []
            for half, axis in enumerate(("x", "y")):
                piece = shards[t][:, half * half_c : (half + 1) * half_c]
                piece = piece if t < 2 else after(piece, tokens[t - 2])
                stacks.append(jnp.stack(ring_gather(piece, axis)))
            first_rings.append(stacks)

    def gather_group(t):
        group_pieces.append([ring_gather(stack, axis) for stack, axis in zip(first_rings[t], ("y", "x"))])

    def weights_in_order(stacks):
        whole = jnp.zeros((TAPS, ny, nx, 2, half_c, half_mid), BF16)
        for half in range(2):
            for second, stack in enumerate(stacks[half]):
                for one in range(stack.shape[0]):
                    back_y, back_x = (second, one) if half == 0 else (one, second)
                    spot = (0, (place_y - back_y) % ny, (place_x - back_x) % nx, half, 0, 0)
                    whole = lax.dynamic_update_slice(whole, stack[one][:, None, None, None], spot)
        return whole.reshape(TAPS, col_c, half_mid)

    ends = cols_n - 1
    gather_first(0)
    started = first_rings[0][0]
    other = swap_cores(canvases)
    left = lax.ppermute(behind(canvases[:, :, -1], started), "col", [(a, a + 1) for a in range(ends)])
    right = lax.ppermute(behind(canvases[:, :, 0], started), "col", [(a + 1, a) for a in range(ends)])
    sides = jnp.stack([left, right])
    other_sides = swap_cores(sides)

    def stacked(mine, theirs, axis):
        return jnp.concatenate([jnp.where(first, mine, theirs), jnp.where(first, theirs, mine)], axis=axis)

    mine_x = (canvases, left, right)
    theirs_x = (other, other_sides[0], other_sides[1])
    parts_x = jnp.stack([canvases, other]).reshape(chip_pixels, channels)

    joined = None
    group_weights = []

    def join(t, joined):
        gather_shard(t + 1)
        gather_shard(t + 2)
        gather_first(t)
        gather_first(t + 1)
        gather_group(t)
        stacks = group_pieces[t]
        if use_kernels:
            ahead = shards[t + 2 : t + 3] + (first_rings[t + 1] if t + 1 < cols_n else [])
            ahead = ahead + ([parts_x] if t == 1 else [])
            joined, weights, token = join_group(
                me, t, cols_n, mine_x, theirs_x, stacks[0] + stacks[1], joined, (ny, nx), ahead
            )
        else:
            source = (col - t) % cols_n
            weights = weights_in_order(stacks)
            part, *edges = [
                lax.dynamic_slice_in_dim(stacked(a, b, 1), source * col_c, col_c, a.ndim - 1)
                for a, b in zip(mine_x, theirs_x)
            ]
            part = jnp.concatenate([edges[0][:, :, None], part, edges[1][:, :, None]], axis=2)
            part = jnp.pad(part, ((0, 0), (1, 1), (0, 0), (0, 0)))
            if joined is None:
                joined = jnp.zeros((canvas_count, tall * width, half_mid), F32)
            for k in range(TAPS):
                view = part[:, k // 3 : k // 3 + tall, k % 3 : k % 3 + width].reshape(joined.shape[:2] + (col_c,))
                joined = joined + jnp.einsum("npc,cm->npm", view, weights[k], preferred_element_type=F32)
            token = jnp.zeros((8, 128), F32)
        group_weights.append(weights)
        tokens.append(token)
        return joined

    slot_level, slot_a, slot_b, slot_second = slot_lists()
    slots = len(slot_level)
    tables = [np.concatenate(axis_tables(c, slot_level)[:2], 2) for c in (slot_a, slot_b)]
    valid = axis_tables(slot_a, slot_level)[2] * axis_tables(slot_b, slot_level)[2]
    counts = [np.sum(axis_tables(c, slot_level)[0], 2) for c in (slot_a, slot_b)]
    counts = np.maximum(counts[0] * counts[1], 1)
    tables = np.concatenate(tables + [valid[:, :, None], counts[:, :, None]], 2).astype(np.float32)
    tables = np.where((slot_second == 1)[None, :, None], tables[:1], tables)
    may_pack = jnp.where(layout[0] == 1, 0, 1)
    tables = behind(jnp.where(layout[may_pack] == 1, tables[1], tables[0]), main_w)
    span = SIDE + 2
    pool_rows, up_rows, pool_cols, up_cols = (tables[:, k * span : (k + 1) * span] for k in range(4))
    mask, counted = tables[:, 4 * span], tables[:, 4 * span + 1]
    on_canvas = jnp.asarray(slot_second)[None, :] == (may_pack != jnp.arange(canvas_count))[:, None]
    on_canvas = on_canvas.astype(F32)
    of_slot = jnp.asarray((slot_level[None, :] == np.arange(LEVELS)[:, None]).astype(np.float32))
    level_mask = of_slot * mask

    def pixel_table(rows, cols):
        table = rows.T[None, :, None, :] * cols.T[None, None, :, :]
        return (on_canvas[:, None, None, :] * table).astype(BF16)

    near_cols = lax.dynamic_slice_in_dim(up_cols, col * width, width + 2, 1)
    up_views = jnp.concatenate(
        [pixel_table(up_rows, near_cols[:, dx : dx + width]) for dx in range(3)], axis=3
    )
    up_flat = jnp.stack(
        [
            pixel_table(lax.dynamic_slice_in_dim(up_rows, 1 + part * height, height, 1), near_cols[:, 1:-1])
            for part in (row, 1 - row)
        ]
    ).reshape(chip_pixels, slots)
    pool_own = pixel_table(
        lax.dynamic_slice_in_dim(pool_rows, 1 + row * height, height, 1),
        lax.dynamic_slice_in_dim(pool_cols, 1 + col * width, width, 1),
    )

    pool_part = jnp.einsum("nyxq,nyxc->qc", pool_own, canvases, preferred_element_type=F32)
    half_channels = channels // rows_n
    mine = lax.dynamic_slice_in_dim(pool_part, row * half_channels, half_channels, 1)
    mine = mine + swap_cores(lax.dynamic_slice_in_dim(pool_part, (1 - row) * half_channels, half_channels, 1))
    mine = jnp.transpose(mine.astype(BF16).reshape(slots, cols_n, group_c), (1, 0, 2))
    pool_sums = jnp.sum(exchange(mine, "col").astype(F32), axis=0)
    joined = join(0, joined)
    pooled = (after(pool_sums, tokens[0]) / counted[:, None]).astype(BF16)

    bw_rows = everyone(behind(branch_w.reshape(own_branch, LEVELS * mid), started), "img")
    bw_rows = bw_rows.reshape(group_c, LEVELS * mid)

    def of_level(wide):
        k = wide.shape[1] // LEVELS
        return sum(of_slot[b][:, None] * wide[:, b * k : (b + 1) * k] for b in range(LEVELS))

    def to_levels(narrow):
        return jnp.concatenate([of_slot[b][:, None].astype(narrow.dtype) * narrow for b in range(LEVELS)], axis=1)

    def slot_rows(per_level):
        return sum(of_slot[b][:, None] * per_level[b][None] for b in range(LEVELS))

    def level_sums(per_slot):
        return jnp.stack([jnp.sum(level_mask[b][:, None] * per_slot, axis=0) for b in range(LEVELS)])

    pre_part = of_level(jnp.dot(pooled, bw_rows, preferred_element_type=F32))
    pre = own_half(pre_part) + swap_cores(lax.dynamic_slice_in_dim(pre_part, (1 - row) * half_mid, half_mid, 1))
    joined = join(1, joined)
    pre = after(sum_over(pre, "col"), tokens[1])
    count_part = jnp.broadcast_to(jnp.sum(level_mask, 1)[:, None], (LEVELS, half_mid))
    stats = sum_over(jnp.concatenate([level_sums(pre), level_sums(pre * pre), count_part]), "img")
    counts = stats[2 * LEVELS :]
    bin_mean = stats[:LEVELS] / counts
    bin_rstd = lax.rsqrt(stats[LEVELS : 2 * LEVELS] / counts - bin_mean * bin_mean + epsilon)
    normed = (pre - slot_rows(bin_mean)) * slot_rows(bin_rstd)
    gain, bias = own_half(branch_gain), own_half(branch_bias)
    feature, gelu_back = jax.vjp(jax.nn.gelu, slot_rows(gain) * normed + slot_rows(bias))
    feature = (mask[:, None] * feature).astype(BF16)
    block_m = half_mid // devices
    by_column = jnp.transpose(after(branch_part, tokens[0]), (0, 2, 1)).reshape(TAPS, cols_n, img_n, block_m, own_join)
    by_column = jnp.transpose(by_column, (1, 2, 0, 3, 4)).reshape(devices, TAPS, block_m, own_join)
    by_column = exchange(by_column, ("col", "img"))
    block_rows = TAPS * block_m
    branch_cols = jnp.transpose(by_column, (1, 2, 0, 3)).reshape(block_rows, LEVELS * mid)

    features = everyone(feature, "img")
    for t in range(2, cols_n - 1):
        joined = join(t, joined)
    other_features = swap_cores(after(features, tokens[-1]))
    if use_kernels:
        cell_w = cell_weights(me, branch_cols, of_slot, features, other_features, tokens[-1])
    else:
        both = jnp.concatenate([jnp.where(first, features, other_features), jnp.where(first, other_features, features)], 2)
        wide = jnp.einsum("rbc,isc->bisr", branch_cols.reshape(block_rows, LEVELS, mid), both, preferred_element_type=F32)
        cell_w = jnp.einsum("bisr,bs->irs", wide, of_slot, precision=lax.Precision.HIGHEST).astype(BF16)
    cell_w = everyone(exchange(cell_w, "img"), "col")
    cell_w = cell_w.reshape(devices, TAPS, block_m, slots)
    cell_w = jnp.transpose(cell_w, (1, 0, 2, 3)).reshape(TAPS, half_mid, slots)

    joined = join(cols_n - 1, joined)
    up_rows_flat = up_views.reshape(canvas_count, (tall + 2) * width, 3 * slots)
    if use_kernels:
        joined, head_sums = join_cells(up_rows_flat, cell_w, joined, width)
    else:
        for k in range(TAPS):
            view = up_rows_flat[:, k // 3 * width : (k // 3 + tall) * width, k % 3 * slots : (k % 3 + 1) * slots]
            joined = joined + jnp.einsum("npq,mq->npm", view, cell_w[k], preferred_element_type=F32)
        head_sums = jnp.stack([jnp.sum(joined, (0, 1)), jnp.sum(joined * joined, (0, 1))])
    joined = joined.reshape(chip_pixels, half_mid)

    def sum_chips(x):
        return sum_over(x, ("col", "img"))

    head_sum = sum_chips(head_sums)
    head_mean = head_sum[0] / total_pixels
    head_rstd = lax.rsqrt(head_sum[1] / total_pixels - head_mean * head_mean + epsilon)
    normed_head = (joined - head_mean) * head_rstd
    head_gain, head_bias = own_half(join_gain), own_half(join_bias)
    activated, head_gelu_back = jax.vjp(jax.nn.gelu, head_gain * normed_head + head_bias)
    act_low = activated.astype(BF16)
    own_class_w = own_half(class_w, 0)
    logits_part = lax.dot_general(
        own_class_w, act_low, (((0,), (1,)), ((), ())), preferred_element_type=F32
    )
    logits = logits_part + swap_cores(logits_part) + class_bias[:, None]
    row_peak = jnp.max(logits, axis=0, keepdims=True)
    exp_terms = jnp.exp(logits - row_peak)
    probabilities = exp_terms / jnp.sum(exp_terms, axis=0, keepdims=True)
    chip_labels = stacked(labels, swap_cores(labels), 1).reshape(1, chip_pixels)
    onehot = (chip_labels == jnp.arange(classes, dtype=jnp.int32)[:, None]).astype(F32)
    dlogits = ((probabilities - onehot) / math.sqrt(total_pixels)).astype(BF16)
    class_part = jnp.dot(dlogits, act_low, preferred_element_type=F32)
    class_bias_part = jnp.sum(dlogits.astype(F32), axis=1)
    grad_act = lax.dot_general(
        dlogits, own_class_w, (((0,), (1,)), ((), ())), preferred_element_type=F32
    )
    grad_head = head_gelu_back(grad_act)[0]
    head_parts = jnp.concatenate(
        [
            jnp.sum(grad_head, 0)[None],
            jnp.sum(grad_head * normed_head, 0)[None],
            class_part,
            jnp.pad(class_bias_part, (0, half_mid - classes))[None],
        ]
    )
    head_totals = sum_chips(head_parts)
    grad_joined = (
        head_gain * head_rstd * (grad_head - (head_totals[0] + normed_head * head_totals[1]) / total_pixels)
    ).astype(BF16).reshape(canvas_count, tall, width, half_mid)
    head_all = both_halves(head_totals)
    grad_join_bias, grad_join_gain = head_all[0], head_all[1]
    grad_class_w = head_all[2 : 2 + classes].T
    grad_class_bias = head_totals[2 + classes, :classes]

    g_left = lax.ppermute(grad_joined[:, :, -1], "col", [(a, a + 1) for a in range(ends)])
    g_right = lax.ppermute(grad_joined[:, :, 0], "col", [(a + 1, a) for a in range(ends)])
    if use_kernels:
        grad_views = gradient_views(
            me, grad_joined.reshape(canvas_count, tall * width, half_mid), g_left, g_right, width
        )
    else:
        wide_grad = jnp.concatenate([g_left[:, :, None], grad_joined, g_right[:, :, None]], axis=2)
        wide_grad = jnp.pad(wide_grad, ((0, 0), (1, 1), (0, 0), (0, 0)))
        grad_views = jnp.concatenate(
            [
                wide_grad[:, 2 - k // 3 : 2 - k // 3 + tall, 2 - k % 3 : 2 - k % 3 + width]
                for k in range(TAPS)
            ],
            axis=3,
        ).reshape(canvas_count, rows_n, height * width, TAPS * half_mid)
        grad_views = jnp.stack(
            [lax.dynamic_index_in_dim(grad_views, part, 1, keepdims=False) for part in (row, 1 - row)]
        )
    flat_views = grad_views.reshape(chip_pixels, TAPS * half_mid)

    received = [[] for _ in range(cols_n)]
    back_tokens, their_grads, mine_grad = [], [], None

    def chunk_of(t):
        dest = (col - 1 - t) % cols_n
        chunk = lax.dynamic_slice_in_dim(parts_x, dest * col_c, col_c, 1)
        chunk = chunk if t < 2 else after(chunk, back_tokens[t - 2])
        part = lax.dot_general(
            chunk, flat_views, (((0,), (0,)), ((), ())), preferred_element_type=F32
        ).astype(BF16)
        part = part.reshape(ny, nx, 2, half_c, TAPS * half_mid)
        done = []
        for half in range(2):
            this = part[:, :, half]
            order = ("x", "y") if half == 0 else ("y", "x")
            dims = {"x": 1, "y": 0}
            place, count = place_on(order[0])
            other = 1 - dims[order[0]]

            def first_block(s, this=this, order=order, place=place, count=count):
                return lax.dynamic_index_in_dim(this, (place - 1 - s) % count, dims[order[0]], keepdims=False)

            line = ring_scatter(first_block, order[0])
            received[t].append(line)
            place2, count2 = place_on(order[1])

            def second_block(s, line=line, place2=place2, count2=count2):
                return lax.dynamic_index_in_dim(line, (place2 - 1 - s) % count2, 0, keepdims=False)

            done.append(ring_scatter(second_block, order[1]))
        return done

    def back(t, ahead):
        nonlocal mine_grad
        if use_kernels:
            theirs, mine_grad, token = back_group(
                me, t, cols_n, grad_views, group_weights[t], mine_grad, channels, ahead
            )
            their_grads.append(swap_cores(theirs))
        else:
            token = jnp.zeros((8, 128), F32)
        back_tokens.append(token)

    chunks = [chunk_of(t) for t in range(min(2, cols_n))]

    cell_grad = lax.dot_general(
        flat_views, up_flat, (((0,), (0,)), ((), ())), preferred_element_type=F32
    ).astype(BF16)
    cell_grad = jnp.transpose(cell_grad.reshape(TAPS, cols_n, img_n, block_m, slots), (1, 2, 0, 3, 4))
    cell_grad = jnp.sum(exchange(cell_grad, "col").astype(F32), axis=0).astype(BF16)
    back(0, received[0])
    chunks.append(chunk_of(2))
    cell_grad = exchange(cell_grad, "img").reshape(img_n, block_rows, slots)
    back(1, received[1] + chunks[0] + [cell_grad])
    chunks.append(chunk_of(3))
    if use_kernels:
        branch_grad, feature_grad, feature_send = cell_back(
            me, branch_cols, of_slot, features, other_features, cell_grad
        )
    else:
        by_level = cell_grad[:, None] * of_slot.astype(BF16)[None, :, None, :]
        branch_grad = jnp.einsum("ibrs,isc->rbc", by_level, both, preferred_element_type=F32).astype(BF16)
        feature_grad = jnp.einsum(
            "ibrs,rbc->isc", by_level, branch_cols.reshape(block_rows, LEVELS, mid), preferred_element_type=F32
        )
        feature_send = lax.dynamic_slice_in_dim(feature_grad, (1 - row) * half_mid, half_mid, 2).astype(BF16)
        feature_grad = own_half(feature_grad)
    feature_grad = (feature_grad + swap_cores(feature_send).astype(F32)).astype(BF16)
    feature_grad = jnp.sum(exchange(feature_grad, "img").astype(F32), axis=0).astype(BF16)
    back(2, received[2] + chunks[1] + [feature_grad])
    for t in range(4, cols_n):
        chunks.append(chunk_of(t))
        back(t - 1, received[t - 1] + chunks[t - 2])
    feature_grad = sum_over(feature_grad, "col")

    back(cols_n - 1, received[cols_n - 1] + chunks[cols_n - 2] + [feature_grad])
    main_grad = ring_scatter(lambda t: jnp.concatenate(chunks[t]), "col").reshape(own_join, TAPS, half_mid)

    branch_grad = jnp.transpose(branch_grad.reshape(block_rows, devices, own_join), (1, 0, 2))
    branch_grad = exchange(after(branch_grad, back_tokens[2]), ("col", "img"))
    branch_grad = branch_grad.reshape(devices, TAPS, block_m, own_join)
    branch_grad = jnp.transpose(branch_grad, (3, 1, 0, 2)).reshape(own_join, TAPS, half_mid)

    sent = swap_cores(jnp.where(first, branch_grad, main_grad))
    kept = jnp.where(first, main_grad, branch_grad)
    grad_join_w = jnp.concatenate([jnp.where(first, kept, sent), jnp.where(first, sent, kept)], axis=2).astype(F32)

    grad_y = gelu_back(feature_grad)[0]
    bin_totals = sum_over(jnp.concatenate([level_sums(grad_y), level_sums(grad_y * normed)]), "img")
    correction = mask[:, None] * (
        slot_rows(bin_totals[:LEVELS] / counts) + normed * slot_rows(bin_totals[LEVELS:] / counts)
    )
    grad_pre = (slot_rows(gain) * slot_rows(bin_rstd) * (grad_y - correction)).astype(BF16)
    grad_pre = to_levels(both_halves(grad_pre))
    bin_totals = both_halves(bin_totals)
    grad_branch_bias, grad_branch_gain = bin_totals[:LEVELS], bin_totals[LEVELS:]

    weight_grad = lax.dot_general(
        pooled, grad_pre, (((0,), (0,)), ((), ())), preferred_element_type=F32
    ).astype(BF16)
    weight_grad = exchange(weight_grad.reshape(img_n, own_branch, LEVELS * mid), "img")
    grad_branch_w = jnp.sum(weight_grad.astype(F32), axis=0).reshape(own_branch, LEVELS, mid)

    grad_pooled = lax.dot_general(grad_pre, bw_rows, (((1,), (1,)), ((), ())), preferred_element_type=F32)
    grad_pooled = (grad_pooled / counted[:, None]).astype(BF16)
    grad_pooled = jnp.transpose(everyone(grad_pooled, "col"), (1, 0, 2)).reshape(slots, half_channels)
    grad_pooled = both_halves(grad_pooled)

    pool_flat = pool_own.reshape(canvas_count, height * width, slots)
    if use_kernels:
        grad_canvases = finish_canvases(
            me, pool_flat, grad_pooled, mine_grad, their_grads
        )
    else:
        grad_canvases = jnp.einsum("npq,qc->npc", pool_flat, grad_pooled, preferred_element_type=F32)
        for t in range(cols_n):
            source = (col - t) % cols_n
            part = jnp.einsum(
                "qnpkm,kcm->qnpc",
                grad_views.reshape(2, canvas_count, -1, TAPS, half_mid),
                group_weights[t],
                preferred_element_type=F32,
            )
            part = part[0] + swap_cores(part[1].astype(BF16)).astype(F32)
            part = part + lax.dynamic_slice_in_dim(grad_canvases, source * col_c, col_c, 2)
            grad_canvases = lax.dynamic_update_slice_in_dim(grad_canvases, part, source * col_c, 2)
    grad_canvases = grad_canvases.reshape(canvases.shape)

    logits = lax.dynamic_slice_in_dim(
        logits.T.reshape(canvas_count, tall, width, classes), row * height, height, 1
    )
    return (
        logits,
        grad_canvases,
        grad_branch_w,
        grad_branch_gain,
        grad_branch_bias,
        grad_join_w,
        grad_join_gain,
        grad_join_bias,
        grad_class_w,
        grad_class_bias,
    )


def solution(mesh):
    in_specs = (
        P("img", "row", "col", None),
        P("img"),
        P("img", "row", "col"),
        P(("row", "col", "img"), None, None),
        P(),
        P(),
        P(("row", "col", "img"), None, None),
        P(),
        P(),
        P(),
        P(),
    )
    out_specs = (
        P("img", "row", "col", None),
        P("img", "row", "col", None),
        P(("row", "col", "img"), None, None),
        P(),
        P(),
        P(("row", "col", "img"), None, None),
        P(),
        P(),
        P(),
        P(),
    )
    return jax.shard_map(
        per_device, mesh=mesh, in_specs=in_specs, out_specs=out_specs, check_vma=False
    )
```

```python
import functools
import math

import jax
import jax.numpy as jnp
import numpy as np
from jax import lax
from jax.experimental import pallas as pl
from jax.experimental.pallas import tpu as pltpu
from jax.sharding import PartitionSpec as P

SIDE = 64
bin_scales = (1, 2, 3, 6)
epsilon = 1e-05
LEVELS = len(bin_scales)
TAPS = 9
BF16 = jnp.bfloat16
F32 = jnp.float32


def slot_lists():
    rows = []
    for level, size in enumerate(bin_scales):
        rows += [(level, a, b, 0) for a in range(2 * size) for b in range(2 * size)]
    for level, size in enumerate(bin_scales):
        rows += [(level, a, b, 1) for a in range(size) for b in range(size)]
    rows += [(-1, 0, 0, 1)] * (-len(rows) % 128)
    return [np.array(column) for column in zip(*rows)]


def axis_tables(cell, level):
    size = np.array(bin_scales)[np.maximum(level, 0)][:, None]
    places = np.arange(SIDE)[None, :]
    pools, ups, valids = [], [], []
    for packed in (0, 1):
        image_side = SIDE // 2 if packed else SIDE
        which_half, in_cell = cell[:, None] // size, cell[:, None] % size
        pixel_half = places // image_side
        local_pos = places - pixel_half * image_side
        usable = ((which_half == 0) | (packed == 1)) & (level[:, None] >= 0)
        same_image = (pixel_half == which_half) & usable
        low_edge = in_cell * image_side // size
        high_edge = ((in_cell + 1) * image_side + size - 1) // size
        inside = same_image & (local_pos >= low_edge) & (local_pos < high_edge)
        numerator = local_pos * (size - 1)
        base_cell = numerator // (image_side - 1)
        fraction = (numerator - base_cell * (image_side - 1)).astype(np.float32) / np.float32(image_side - 1)
        weight = np.where(in_cell == base_cell, np.float32(1) - fraction, np.float32(0))
        weight = weight + np.where(in_cell == base_cell + 1, fraction, np.float32(0))
        weight = np.where(same_image, weight, np.float32(0)).astype(np.float32)
        pad = ((0, 0), (1, 1))
        pools.append(np.pad(inside.astype(np.float32), pad))
        ups.append(np.pad(weight, pad))
        valids.append(usable[:, 0].astype(np.float32))
    return np.stack(pools), np.stack(ups), np.stack(valids)


def swap_cores(x):
    return lax.ppermute(x, "row", [(0, 1), (1, 0)])


def exchange(blocks, axis):
    return lax.all_to_all(blocks, axis, 0, 0, tiled=True)


def everyone(x, axis):
    return exchange(jnp.broadcast_to(x[None], (lax.axis_size(axis),) + x.shape), axis)


def partner(x, step):
    count = lax.axis_size("img")
    return lax.ppermute(x, "img", [(a, a ^ step) for a in range(count)])


def scatter(blocks, axis):
    me, count = lax.axis_index(axis), lax.axis_size(axis)
    parts = [lax.dynamic_index_in_dim(blocks, me ^ s, 0, keepdims=False) for s in range(count)]
    return [parts[0]] + [
        lax.ppermute(parts[s], axis, [(a, a ^ s) for a in range(count)]) for s in range(1, count)
    ]


def sum_over(x, axis):
    return jnp.sum(everyone(x, axis).astype(F32), axis=0)


def ring_gather(x, axis):
    count = lax.axis_size(axis)
    parts = [x]
    for _ in range(count - 1):
        parts.append(lax.ppermute(parts[-1], axis, [(a, (a + 1) % count) for a in range(count)]))
    return parts


def ring_scatter(block_of, axis):
    count = lax.axis_size(axis)
    totals = [block_of(0)]
    for t in range(1, count):
        total = lax.ppermute(totals[-1], axis, [(a, (a + 1) % count) for a in range(count)])
        totals.append((total.astype(F32) + block_of(t).astype(F32)).astype(BF16))
    return totals


VMEM_LIMIT = 56 << 20


def cost(microseconds):
    return pl.CostEstimate(
        flops=int(microseconds * 2.8e9), bytes_accessed=int(microseconds * 9e6), transcendentals=0
    )


ANYWHERE = pl.BlockSpec(memory_space=pl.ANY)
BESIDE = 16 + 16


def whole(a, buffers=None):
    mode = {} if buffers is None else {"pipeline_mode": pl.Buffered(buffers)}
    return pl.BlockSpec(a.shape, lambda *_, r=len(a.shape): (0,) * r, **mode)


def pack_kernel(me, *refs, groups):
    sources, outs = refs[:4], refs[5:]
    lanes = outs[0].shape[2] // groups
    start = 0
    for ref in sources:
        size = ref.shape[1]
        for s, out_ref in enumerate(outs):
            for j in range(groups):
                at = pl.ds(pl.multiple_of((j * len(outs) + (me[2] ^ s)) * lanes, lanes), lanes)
                out_ref[0, start : start + size, j * lanes : (j + 1) * lanes] = ref[0, :, at]
        start += size


def pack(me, tile, left, right, line, blocks, groups, ahead):
    count, _, channels = tile.shape
    sources = (tile, left, right, line)
    rows = sum(x.shape[1] for x in sources)
    depth = channels // blocks
    return pl.pallas_call(
        functools.partial(pack_kernel, groups=groups),
        grid_spec=pltpu.PrefetchScalarGridSpec(
            num_scalar_prefetch=1,
            grid=(count,),
            in_specs=[pl.BlockSpec((1,) + x.shape[1:], lambda n, p: (n, 0, 0)) for x in sources] + [ANYWHERE],
            out_specs=[pl.BlockSpec((1, rows, depth), lambda n, p: (n, 0, 0))] * blocks,
        ),
        out_shape=[jax.ShapeDtypeStruct((count, rows, depth), tile.dtype)] * blocks,
        compiler_params=pltpu.CompilerParams(vmem_limit_bytes=VMEM_LIMIT),
        cost_estimate=cost(5),
        name="pack",
    )(me, *sources, ahead)


def lay_rows(rows_ref, wide_ref, row, pixels, left, right, beside, height, width):
    depth = rows_ref.shape[1] // 3
    rows = wide_ref.shape[0]
    for lane in range(0, depth, 128):
        at = slice(lane, lane + 128)
        edge = beside(0, width, at).astype(F32)
        corners = beside(width, 16, at).astype(F32)
        wide_ref[1 : height + 1, 8 : 8 + width] = pixels(at).astype(F32).reshape(height, width, 128)
        flat = wide_ref.reshape(rows * 32, 128)
        flat[pl.ds(32 + 7, height, stride=32)] = left(at).astype(F32)
        flat[pl.ds(32 + 8 + width, height, stride=32)] = right(at).astype(F32)
        for start, there in ((0, row == 1), ((height + 1) * 32, row == 0)):
            flat[start + 8 : start + 8 + width] = jnp.where(there, edge, 0.0)
            flat[start + 7 : start + 8] = jnp.where(there, corners[0:1], 0.0)
            flat[start + 8 + width : start + 9 + width] = jnp.where(there, corners[1:2], 0.0)
        for shift in range(3):
            view = wide_ref[:, 7 + shift : 7 + shift + width].reshape(rows * width, 128)
            rows_ref[:, shift * depth + lane : shift * depth + lane + 128] = view.astype(BF16)


def lay_tile(rows_ref, wide_ref, row, tile_ref, height, width):
    pixels = height * width

    def part(first, size):
        return lambda at: tile_ref[0, first : first + size, at]

    def beside(start, size, at):
        return tile_ref[0, pixels + 2 * height + start : pixels + 2 * height + start + size, at]

    lay_rows(
        rows_ref,
        wide_ref,
        row,
        part(0, pixels),
        part(pixels, height),
        part(pixels + height, height),
        beside,
        height,
        width,
    )


def wide_scratch(height):
    return pltpu.VMEM((height + 2, 32, 128), F32)


def join_kernel(me, x_ref, *refs, height, width, have, extra):
    if have:
        w_ref, (out_ref, flip_ref, rows_ref, wide_ref) = refs[0], refs[1 + extra :]
    else:
        mine_ref, theirs_ref = refs[:2]
        out_ref, flip_ref, w_ref, token_ref, rows_ref, wide_ref = refs[2 + extra :]
        groups, _, rows, half = mine_ref.shape

        @pl.when(pl.program_id(0) == 0)
        def _():
            token_ref[...] = jnp.zeros(token_ref.shape, F32)
            for t in range(groups):
                start = pl.multiple_of((me[1] + groups - t) % groups * rows, rows)
                for ref, side in ((mine_ref, me[0]), (theirs_ref, 1 - me[0])):
                    w_ref[:, pl.ds(start, rows), pl.ds(pl.multiple_of(side * half, half), half)] = ref[t]

    depth = x_ref.shape[-1]
    lay_tile(rows_ref, wide_ref, me[0], x_ref, height, width)
    flip_ref[0] = x_ref[0, : height * width].T
    total = jnp.zeros(out_ref.shape[1:], F32)
    for dy in range(3):
        total = total + jnp.dot(
            rows_ref[dy * width : (dy + height) * width],
            w_ref[3 * dy : 3 * dy + 3].reshape(3 * depth, -1),
            preferred_element_type=F32,
        )
    out_ref[0] = total.astype(out_ref.dtype)


def join_tiles(me, x, weights, height, width, dtype, ahead=()):
    count, _, depth = x.shape
    pixels = height * width
    have = not isinstance(weights, tuple)
    if have:
        weights = (weights,)
        taps, m = weights[0].shape[0], weights[0].shape[2]
    else:
        taps, m = weights[0].shape[1], 2 * weights[0].shape[3]
    out = jax.ShapeDtypeStruct((count, pixels, m), dtype)
    made = jax.ShapeDtypeStruct((taps, depth, m), BF16)
    token = jax.ShapeDtypeStruct((8, 128), F32)
    flip = jax.ShapeDtypeStruct((count, depth, pixels), BF16)
    out_spec = [
        pl.BlockSpec((1, pixels, m), lambda n, p: (n, 0, 0)),
        pl.BlockSpec((1, depth, pixels), lambda n, p: (n, 0, 0)),
    ]
    return pl.pallas_call(
        functools.partial(join_kernel, height=height, width=width, have=have, extra=len(ahead)),
        grid_spec=pltpu.PrefetchScalarGridSpec(
            num_scalar_prefetch=1,
            grid=(count,),
            in_specs=[pl.BlockSpec((1,) + x.shape[1:], lambda n, p: (n, 0, 0))]
            + [whole(w, 1) for w in weights]
            + [ANYWHERE] * len(ahead),
            out_specs=out_spec + ([] if have else [whole(made, 1), whole(token)]),
            scratch_shapes=[pltpu.VMEM(((height + 2) * width, 3 * depth), BF16), wide_scratch(height)],
        ),
        out_shape=[out, flip] + ([] if have else [made, token]),
        compiler_params=pltpu.CompilerParams(vmem_limit_bytes=VMEM_LIMIT),
        cost_estimate=cost(8),
        name="join_tiles",
    )(me, x, *weights, *ahead)


def cells_kernel(me, up_ref, mine_ref, theirs_ref, *refs, height, width):
    parts, (out_ref, sums_ref) = refs[:-2], refs[-2:]
    slots = mine_ref.shape[2]
    half = mine_ref.shape[1]
    for ref, side in ((mine_ref, me[0]), (theirs_ref, 1 - me[0])):
        total = jnp.zeros((height * width, half), F32)
        for k in range(TAPS):
            dy, dx = k // 3, k % 3
            total = total + lax.dot_general(
                up_ref[0, dy * width : (dy + height) * width, dx * slots : (dx + 1) * slots],
                ref[k],
                (((1,), (1,)), ((), ())),
                preferred_element_type=F32,
            )
        out_ref[0, :, pl.ds(pl.multiple_of(side * half, half), half)] = total
    total = out_ref[0]
    for part_ref in parts:
        total = total + part_ref[0].astype(F32)
    out_ref[0] = total

    @pl.when(pl.program_id(0) == 0)
    def _():
        sums_ref[...] = jnp.zeros(sums_ref.shape, F32)

    sums_ref[0:1] += jnp.sum(total, 0, keepdims=True)
    sums_ref[1:2] += jnp.sum(total * total, 0, keepdims=True)


def join_cells(me, up, mine, theirs, parts, height, width):
    count, pixels, m = parts[0].shape
    return pl.pallas_call(
        functools.partial(cells_kernel, height=height, width=width),
        grid_spec=pltpu.PrefetchScalarGridSpec(
            num_scalar_prefetch=1,
            grid=(count,),
            in_specs=[pl.BlockSpec((1,) + up.shape[1:], lambda n, p: (n, 0, 0)), whole(mine), whole(theirs)]
            + [pl.BlockSpec((1, pixels, m), lambda n, p: (n, 0, 0))] * len(parts),
            out_specs=[
                pl.BlockSpec((1, pixels, m), lambda n, p: (n, 0, 0)),
                pl.BlockSpec((2, m), lambda n, p: (0, 0)),
            ],
        ),
        out_shape=[jax.ShapeDtypeStruct((count, pixels, m), F32), jax.ShapeDtypeStruct((2, m), F32)],
        compiler_params=pltpu.CompilerParams(vmem_limit_bytes=VMEM_LIMIT),
        cost_estimate=cost(6),
        name="join_cells",
    )(me, up, mine, theirs, *parts)


def tap_rows(rows_ref, k, height, width):
    m = rows_ref.shape[1] // 3
    dy, dx = 2 - k // 3, 2 - k % 3
    return rows_ref[dy * width : (dy + height) * width, dx * m : (dx + 1) * m]


def cells_back_kernel(me, g_ref, up_ref, mine_ref, theirs_ref, total_ref, rows_ref, wide_ref, *, height, width):
    lay_tile(rows_ref, wide_ref, me[0], g_ref, height, width)
    half = mine_ref.shape[1]
    count = pl.num_programs(0)
    cells = up_ref[0].T

    @pl.when(pl.program_id(0) == 0)
    def _():
        total_ref[...] = jnp.zeros(total_ref.shape, F32)

    for k in range(TAPS):
        total_ref[k] += jnp.dot(cells, tap_rows(rows_ref, k, height, width), preferred_element_type=F32)

    @pl.when(pl.program_id(0) == count - 1)
    def _():
        for k in range(TAPS):
            for ref, side in ((mine_ref, me[0]), (theirs_ref, 1 - me[0])):
                ref[k] = total_ref[k, :, pl.ds(pl.multiple_of(side * half, half), half)].T.astype(BF16)


def cells_gradient(me, g, up, height, width):
    count, rows, m = g.shape
    slots = up.shape[2]
    out = jax.ShapeDtypeStruct((TAPS, m // 2, slots), BF16)
    return pl.pallas_call(
        functools.partial(cells_back_kernel, height=height, width=width),
        grid_spec=pltpu.PrefetchScalarGridSpec(
            num_scalar_prefetch=1,
            grid=(count,),
            in_specs=[
                pl.BlockSpec((1, rows, m), lambda n, p: (n, 0, 0)),
                pl.BlockSpec((1,) + up.shape[1:], lambda n, p: (n, 0, 0)),
            ],
            out_specs=[whole(out), whole(out)],
            scratch_shapes=[
                pltpu.VMEM((TAPS, slots, m), F32),
                pltpu.VMEM(((height + 2) * width, 3 * m), BF16),
                wide_scratch(height),
            ],
        ),
        out_shape=[out, out],
        compiler_params=pltpu.CompilerParams(vmem_limit_bytes=VMEM_LIMIT),
        cost_estimate=cost(6),
        name="cells_gradient",
    )(me, g, up)


def by_pixels_kernel(me, g_ref, w_ref, *refs, height, width):
    dx_ref, token_ref, rows_ref, wide_ref = refs[-4:]
    lay_tile(rows_ref, wide_ref, me[0], g_ref, height, width)
    token_ref[...] = jnp.zeros(token_ref.shape, F32)
    total = jnp.zeros(dx_ref.shape[1:], F32)
    for k in range(TAPS):
        total = total + lax.dot_general(
            tap_rows(rows_ref, k, height, width), w_ref[k], (((1,), (1,)), ((), ())), preferred_element_type=F32
        )
    dx_ref[0] = total.astype(dx_ref.dtype)


def by_pixels(me, g, weights, height, width, dtype, ahead=()):
    count, rows, m = g.shape
    depth = weights.shape[1]
    return pl.pallas_call(
        functools.partial(by_pixels_kernel, height=height, width=width),
        grid_spec=pltpu.PrefetchScalarGridSpec(
            num_scalar_prefetch=1,
            grid=(count,),
            in_specs=[pl.BlockSpec((1, rows, m), lambda n, p: (n, 0, 0)), whole(weights, 1)]
            + [ANYWHERE] * len(ahead),
            out_specs=[
                pl.BlockSpec((1, height * width, depth), lambda n, p: (n, 0, 0)),
                pl.BlockSpec((8, 128), lambda n, p: (0, 0)),
            ],
            scratch_shapes=[pltpu.VMEM(((height + 2) * width, 3 * m), BF16), wide_scratch(height)],
        ),
        out_shape=[
            jax.ShapeDtypeStruct((count, height * width, depth), dtype),
            jax.ShapeDtypeStruct((8, 128), F32),
        ],
        compiler_params=pltpu.CompilerParams(vmem_limit_bytes=VMEM_LIMIT),
        cost_estimate=cost(9),
        name="by_pixels",
    )(me, g, weights, *ahead)


def by_weights_kernel(me, *refs, height, width, tiles):
    g_refs, x_refs = refs[:tiles], refs[tiles : 2 * tiles]
    out_ref, token_ref, rows_ref, wide_ref, x_ref, total_ref = refs[-6:]
    step = pl.program_id(0)
    count = g_refs[0].shape[0]
    pixels = height * width
    for s in range(tiles):

        @pl.when(step == s)
        def _(s=s):
            for n in range(count):
                lay_tile(rows_ref.at[n], wide_ref, me[0], g_refs[s].at[pl.ds(n, 1)], height, width)
                x_ref[:, n * pixels : (n + 1) * pixels] = x_refs[s][n]

    @pl.when(step == 0)
    def _():
        total_ref[...] = jnp.zeros(total_ref.shape, F32)

    for k in range(TAPS):
        for n in range(count):
            total_ref[k] += jnp.dot(
                x_ref[:, n * pixels : (n + 1) * pixels],
                tap_rows(rows_ref.at[n], k, height, width),
                preferred_element_type=F32,
            )

    @pl.when(step == tiles - 1)
    def _():
        token_ref[...] = jnp.zeros(token_ref.shape, F32)
        groups, _, rows, _ = out_ref.shape
        for j in range(groups):
            out_ref[j] = total_ref[:, j * rows : (j + 1) * rows].astype(BF16)


def by_weights(me, own, gs, xs, groups, height, width, ahead=()):
    tiles = len(gs)
    count, rows, m = gs[0].shape
    depth = xs[0].shape[1]
    out = jax.ShapeDtypeStruct((groups, TAPS, depth // groups, m // 2), BF16)
    token = jax.ShapeDtypeStruct((8, 128), F32)
    half = pl.BlockSpec(
        (count, rows, m // 2), lambda s, p: (0, 0, p[0] if own else 1 - p[0]), pipeline_mode=pl.Buffered(1)
    )
    return pl.pallas_call(
        functools.partial(by_weights_kernel, height=height, width=width, tiles=tiles),
        grid_spec=pltpu.PrefetchScalarGridSpec(
            num_scalar_prefetch=1,
            grid=(tiles,),
            in_specs=[half] * tiles + [whole(x, 1) for x in xs] + [ANYWHERE] * len(ahead),
            out_specs=[whole(out, 1), whole(token)],
            scratch_shapes=[
                pltpu.VMEM((count, (height + 2) * width, 3 * m // 2), BF16),
                wide_scratch(height),
                pltpu.VMEM((depth, count * height * width), BF16),
                pltpu.VMEM((TAPS, depth, m // 2), F32),
            ],
        ),
        out_shape=[out, token],
        compiler_params=pltpu.CompilerParams(vmem_limit_bytes=VMEM_LIMIT),
        cost_estimate=cost(20),
        name="by_weights",
    )(me, *gs, *xs, *ahead)


def finish_kernel(me, pool_ref, cells_ref, *refs, groups):
    parts, out_ref, sum_ref = refs[:-2], refs[-2], refs[-1]
    lanes = parts[0].shape[2] // groups
    for s, ref in enumerate(parts):
        for j in range(groups):
            at = pl.ds(pl.multiple_of((j * len(parts) + (me[2] ^ s)) * lanes, lanes), lanes)
            sum_ref[:, at] = ref[0, :, j * lanes : (j + 1) * lanes]
    depth = parts[0].shape[2]
    for c in range(0, out_ref.shape[2], depth):
        at = slice(c, c + depth)
        out_ref[0, :, at] = sum_ref[:, at].astype(F32) + jnp.dot(
            pool_ref[0], cells_ref[:, at], preferred_element_type=F32
        )


def finish_canvases(me, pool, cells, parts, groups):
    count, pixels, slots = pool.shape
    channels = cells.shape[1]
    return pl.pallas_call(
        functools.partial(finish_kernel, groups=groups),
        grid_spec=pltpu.PrefetchScalarGridSpec(
            num_scalar_prefetch=1,
            grid=(count,),
            in_specs=[pl.BlockSpec((1, pixels, slots), lambda n, p: (n, 0, 0)), whole(cells)]
            + [pl.BlockSpec((1,) + part.shape[1:], lambda n, p: (n, 0, 0)) for part in parts],
            out_specs=pl.BlockSpec((1, pixels, channels), lambda n, p: (n, 0, 0)),
            scratch_shapes=[pltpu.VMEM((pixels, channels), BF16)],
        ),
        out_shape=jax.ShapeDtypeStruct((count, pixels, channels), F32),
        compiler_params=pltpu.CompilerParams(vmem_limit_bytes=VMEM_LIMIT),
        cost_estimate=cost(8),
        name="finish_canvases",
    )(me, pool, cells, *parts)


def all_features(me, feat_ref, mine_ref, theirs_ref):
    half = mine_ref.shape[1]
    for ref, side in ((mine_ref, me[0]), (theirs_ref, 1 - me[0])):
        feat_ref[:, pl.ds(pl.multiple_of(side * half, half), half)] = ref[...]


def cell_weights_kernel(me, level_ref, mine_ref, theirs_ref, *refs, parts):
    cols, (out_ref, feat_ref) = refs[:parts], refs[-2:]
    all_features(me, feat_ref, mine_ref, theirs_ref)
    total = jnp.zeros(out_ref.shape, F32)
    for b in range(LEVELS):
        part = jnp.zeros(out_ref.shape, F32)
        for t, ref in enumerate(cols):
            lanes = ref.shape[2]
            feat = feat_ref[:, pl.ds(pl.multiple_of((me[2] ^ t) * lanes, lanes), lanes)]
            part = part + lax.dot_general(ref[b], feat, (((1,), (1,)), ((), ())), preferred_element_type=F32)
        total = total + level_ref[b : b + 1, :] * part
    out_ref[...] = total.astype(BF16)


def cell_weights(me, cols, of_slot, mine, theirs, ahead):
    slots, half = mine.shape
    out = jax.ShapeDtypeStruct((cols[0].shape[1], slots), BF16)
    return pl.pallas_call(
        functools.partial(cell_weights_kernel, parts=len(cols)),
        grid_spec=pltpu.PrefetchScalarGridSpec(
            num_scalar_prefetch=1,
            grid=(1,),
            in_specs=[whole(of_slot), whole(mine), whole(theirs)] + [whole(c) for c in cols] + [ANYWHERE],
            out_specs=whole(out),
            scratch_shapes=[pltpu.VMEM((slots, 2 * half), BF16)],
        ),
        out_shape=out,
        compiler_params=pltpu.CompilerParams(vmem_limit_bytes=VMEM_LIMIT),
        cost_estimate=cost(4),
        name="cell_weights",
    )(me, of_slot, mine, theirs, *cols, ahead)


def cell_back_kernel(me, level_ref, mine_ref, theirs_ref, grad_ref, *refs, parts):
    cols, col_grads = refs[:parts], refs[parts : 2 * parts]
    own_ref, send_ref, feat_ref, back_ref = refs[2 * parts :]
    all_features(me, feat_ref, mine_ref, theirs_ref)
    half = mine_ref.shape[1]
    grads = [grad_ref[...] * level_ref[b : b + 1, :].astype(BF16) for b in range(LEVELS)]
    for t, (ref, out_ref) in enumerate(zip(cols, col_grads)):
        lanes = ref.shape[2]
        at = pl.ds(pl.multiple_of((me[2] ^ t) * lanes, lanes), lanes)
        total = jnp.zeros((mine_ref.shape[0], lanes), F32)
        for b in range(LEVELS):
            out_ref[b] = jnp.dot(grads[b], feat_ref[:, at], preferred_element_type=F32).astype(BF16)
            total = total + lax.dot_general(
                grads[b], ref[b], (((0,), (0,)), ((), ())), preferred_element_type=F32
            )
        back_ref[:, at] = total
    for ref, side in ((own_ref, me[0]), (send_ref, 1 - me[0])):
        ref[...] = back_ref[:, pl.ds(pl.multiple_of(side * half, half), half)].astype(ref.dtype)


def cell_back(me, cols, of_slot, mine, theirs, grad):
    slots, half = mine.shape
    outs = [jax.ShapeDtypeStruct(c.shape, BF16) for c in cols]
    outs += [jax.ShapeDtypeStruct(mine.shape, F32), jax.ShapeDtypeStruct(mine.shape, BF16)]
    *col_grads, own, send = pl.pallas_call(
        functools.partial(cell_back_kernel, parts=len(cols)),
        grid_spec=pltpu.PrefetchScalarGridSpec(
            num_scalar_prefetch=1,
            grid=(1,),
            in_specs=[whole(a) for a in (of_slot, mine, theirs, grad)] + [whole(c) for c in cols],
            out_specs=[whole(a) for a in outs],
            scratch_shapes=[pltpu.VMEM((slots, 2 * half), BF16), pltpu.VMEM((slots, 2 * half), F32)],
        ),
        out_shape=outs,
        compiler_params=pltpu.CompilerParams(vmem_limit_bytes=VMEM_LIMIT),
        cost_estimate=cost(5),
        name="cell_back",
    )(me, of_slot, mine, theirs, grad, *cols)
    return col_grads, own, send


def per_device(
    canvases,
    layout,
    labels,
    branch_w,
    branch_gain,
    branch_bias,
    join_w,
    join_gain,
    join_bias,
    class_w,
    class_bias,
):
    canvas_count, height, width, channels = canvases.shape
    mid = join_w.shape[2]
    half_mid = mid // 2
    classes = class_w.shape[1]
    own_join = join_w.shape[0]
    own_branch = branch_w.shape[0]
    row, col, img = lax.axis_index("row"), lax.axis_index("col"), lax.axis_index("img")
    rows_n, cols_n, img_n = lax.axis_size("row"), lax.axis_size("col"), lax.axis_size("img")
    tall = height * rows_n
    pixels = height * width
    own_pixels = canvas_count * pixels
    total_pixels = own_pixels * rows_n * cols_n * img_n
    devices = cols_n * img_n
    group = row * cols_n + col
    group_c = channels // (rows_n * cols_n)
    depth = channels // img_n
    first = row == 0
    use_kernels = width == 16 and height % 16 == 0 and own_join % 128 == 0 and img_n == 4

    def own_half(x, axis=-1):
        return lax.dynamic_slice_in_dim(x, row * half_mid, half_mid, axis)

    def both_halves(x, axis=-1):
        other = swap_cores(x)
        return jnp.concatenate([jnp.where(first, x, other), jnp.where(first, other, x)], axis=axis)

    taps_first = jnp.transpose(join_w, (1, 0, 2))
    kept = own_half(taps_first)
    swapped = swap_cores(lax.dynamic_slice_in_dim(taps_first, (1 - row) * half_mid, half_mid, 2))
    main_w = jnp.where(first, kept, swapped)
    branch_part = jnp.where(first, swapped, kept)

    me = jnp.stack([row, col, img]).astype(jnp.int32)

    def after(x, token):
        return x + token[0, 0].astype(x.dtype)

    def behind(x, *others):
        if not others:
            return x
        return x + sum((other[(0,) * other.ndim] * 0).astype(F32) for other in others).astype(x.dtype)

    ends = cols_n - 1
    left = lax.ppermute(canvases[:, :, -1], "col", [(a, a + 1) for a in range(ends)])
    right = lax.ppermute(canvases[:, :, 0], "col", [(a + 1, a) for a in range(ends)])
    shards_list = ring_gather(behind(main_w, left, right), "col")
    shards = jnp.stack(shards_list)

    def edges(tile):
        left = lax.ppermute(tile[:, :, -1], "col", [(a, a + 1) for a in range(ends)])
        right = lax.ppermute(tile[:, :, 0], "col", [(a + 1, a) for a in range(ends)])
        return left, right

    def beside_row(tile, left, right):
        edge = jnp.where(first, height - 1, 0)
        line = lax.dynamic_index_in_dim(tile, edge, 1, keepdims=False)
        corners = [lax.dynamic_slice_in_dim(side, edge, 1, 1) for side in (left, right)]
        line = jnp.concatenate([line] + corners + [jnp.zeros_like(line[:, :1])] * (BESIDE - width - 2), axis=1)
        return swap_cores(line)

    def windows(tile):
        left, right = (tile[:, pixels + k * height : pixels + (k + 1) * height] for k in range(2))
        line = tile[:, pixels + 2 * height :]
        tile = tile[:, :pixels].reshape(-1, height, width, tile.shape[2])
        wide = jnp.concatenate([left[:, :, None], tile, right[:, :, None]], axis=2)
        line = jnp.concatenate([line[:, width : width + 1], line[:, :width], line[:, width + 1 : width + 2]], axis=1)
        line = line[:, None]
        wide = jnp.concatenate([jnp.where(first, 0, line), wide, jnp.where(first, line, 0)], axis=1)
        return [
            wide[:, k // 3 : k // 3 + height, k % 3 : k % 3 + width].reshape(-1, pixels, wide.shape[3])
            for k in range(TAPS)
        ]

    surround = (canvases.reshape(canvas_count, pixels, channels), left, right, beside_row(canvases, left, right))
    if use_kernels:
        tiles = pack(me, *surround, img_n, cols_n, main_w)
    else:
        by_block = jnp.concatenate(surround, axis=1).reshape(canvas_count, -1, cols_n, img_n, own_join)
        tiles = [
            lax.dynamic_index_in_dim(by_block, img ^ s, 3, keepdims=False).reshape(canvas_count, -1, depth)
            for s in range(img_n)
        ]
    packed = tiles[0]
    tiles = [packed] + [partner(tiles[s], s) for s in range(1, img_n)]

    other_shards = swap_cores(behind(shards, *tiles[1:3]))

    if not use_kernels:
        weights = jnp.zeros((TAPS, cols_n, own_join, 2, half_mid), BF16)
        for t in range(cols_n):
            for shard, side in ((shards[t], row), (other_shards[t], 1 - row)):
                spot = (0, (col - t) % cols_n, 0, side, 0)
                weights = lax.dynamic_update_slice(weights, shard[:, None, :, None], spot)
        weights = weights.reshape(TAPS, depth, mid)
    shares, made, flips = [], [], []
    for s in range(img_n):
        dtype = F32 if s == 0 else BF16
        if use_kernels and s == 0:
            share, flip, weights, token = join_tiles(me, tiles[s], (shards, other_shards), height, width, dtype)
            flips.append(flip)
        elif use_kernels:
            share, flip = join_tiles(me, tiles[s], weights, height, width, dtype)
            flips.append(flip)
        else:
            share = jnp.zeros((canvas_count, pixels, mid), F32)
            for k, window in enumerate(windows(tiles[s])):
                share = share + jnp.einsum("npc,cm->npm", window, weights[k], preferred_element_type=F32)
            share = share.astype(dtype)
            token = jnp.zeros((8, 128), F32)
        made.append(share)
        shares.append(share if s == 0 else partner(share, s))

    bw_rows = everyone(behind(branch_w.reshape(own_branch, LEVELS * mid), main_w), "img")
    bw_rows = bw_rows.reshape(group_c, LEVELS * mid)


    slot_level, slot_a, slot_b, slot_second = slot_lists()
    slots = len(slot_level)
    tables = [np.concatenate(axis_tables(c, slot_level)[:2], 2) for c in (slot_a, slot_b)]
    valid = axis_tables(slot_a, slot_level)[2] * axis_tables(slot_b, slot_level)[2]
    counts = [np.sum(axis_tables(c, slot_level)[0], 2) for c in (slot_a, slot_b)]
    counts = np.maximum(counts[0] * counts[1], 1)
    tables = np.concatenate(tables + [valid[:, :, None], counts[:, :, None]], 2).astype(np.float32)
    tables = np.where((slot_second == 1)[None, :, None], tables[:1], tables)
    may_pack = jnp.where(layout[0] == 1, 0, 1)
    tables = behind(jnp.where(layout[may_pack] == 1, tables[1], tables[0]), packed, shards_list[2], bw_rows)
    span = SIDE + 2
    pool_rows, up_rows, pool_cols, up_cols = (tables[:, k * span : (k + 1) * span] for k in range(4))
    mask, counted = tables[:, 4 * span], tables[:, 4 * span + 1]
    on_canvas = jnp.asarray(slot_second)[None, :] == (may_pack != jnp.arange(canvas_count))[:, None]
    on_canvas = on_canvas.astype(F32)
    of_slot = jnp.asarray((slot_level[None, :] == np.arange(LEVELS)[:, None]).astype(np.float32))
    level_mask = of_slot * mask

    def pixel_table(rows, cols):
        table = rows.T[None, :, None, :] * cols.T[None, None, :, :]
        return (on_canvas[:, None, None, :] * table).astype(BF16)

    def own_rows(table, margin):
        return lax.dynamic_slice_in_dim(table, 1 + row * height - margin, height + 2 * margin, 1)

    near_cols = lax.dynamic_slice_in_dim(up_cols, col * width, width + 2, 1)
    up_views = jnp.concatenate(
        [pixel_table(own_rows(up_rows, 1), near_cols[:, dx : dx + width]) for dx in range(3)], axis=3
    ).reshape(canvas_count, (height + 2) * width, 3 * slots)
    up_own = pixel_table(own_rows(up_rows, 0), near_cols[:, 1:-1]).reshape(canvas_count, pixels, slots)
    pool_own = pixel_table(
        own_rows(pool_rows, 0),
        lax.dynamic_slice_in_dim(pool_cols, 1 + col * width, width, 1),
    )

    pool_part = jnp.einsum("nyxq,nyxc->qc", pool_own, canvases, preferred_element_type=F32)
    half_channels = channels // rows_n
    mine = lax.dynamic_slice_in_dim(pool_part, row * half_channels, half_channels, 1)
    mine = mine + swap_cores(lax.dynamic_slice_in_dim(pool_part, (1 - row) * half_channels, half_channels, 1))
    mine = behind(mine, shards_list[-1])
    mine = jnp.transpose(mine.astype(BF16).reshape(slots, cols_n, group_c), (1, 0, 2))
    pool_sums = jnp.sum(exchange(mine, "col").astype(F32), axis=0)
    block_m = half_mid // cols_n
    block_rows = TAPS * block_m
    by_column = jnp.transpose(branch_part, (0, 2, 1)).reshape(TAPS, cols_n, block_m, own_join)
    by_column = jnp.transpose(by_column, (1, 0, 2, 3)).reshape(cols_n, block_rows, own_join)
    by_column = exchange(behind(by_column, pool_sums), "col")
    branch_cols = [by_column] + [partner(by_column, t) for t in range(1, img_n)]

    def plain_cols(parts):
        out = jnp.zeros((img_n,) + parts[0].shape, parts[0].dtype)
        for t, part in enumerate(parts):
            out = lax.dynamic_update_slice(out, part[None], (img ^ t, 0, 0, 0))
        return jnp.transpose(out, (2, 1, 0, 3)).reshape(block_rows, LEVELS, mid)

    pool_sums = after(pool_sums, token)
    pooled = (pool_sums / counted[:, None]).astype(BF16)

    def of_level(wide):
        k = wide.shape[1] // LEVELS
        return sum(of_slot[b][:, None] * wide[:, b * k : (b + 1) * k] for b in range(LEVELS))

    def to_levels(narrow):
        return jnp.concatenate([of_slot[b][:, None].astype(narrow.dtype) * narrow for b in range(LEVELS)], axis=1)

    def slot_rows(per_level):
        return sum(of_slot[b][:, None] * per_level[b][None] for b in range(LEVELS))

    def level_sums(per_slot):
        return jnp.stack([jnp.sum(level_mask[b][:, None] * per_slot, axis=0) for b in range(LEVELS)])

    pre_part = of_level(jnp.dot(pooled, bw_rows, preferred_element_type=F32))
    pre = own_half(pre_part) + swap_cores(lax.dynamic_slice_in_dim(pre_part, (1 - row) * half_mid, half_mid, 1))
    pre = sum_over(behind(pre, by_column).astype(BF16), "col")
    pre = behind(pre, made[1])
    count_part = jnp.broadcast_to(jnp.sum(level_mask, 1)[:, None], (LEVELS, half_mid))
    stats = sum_over(jnp.concatenate([level_sums(pre), level_sums(pre * pre), count_part]), "img")
    stats = behind(stats, made[2], tiles[3])
    counts = stats[2 * LEVELS :]
    bin_mean = stats[:LEVELS] / counts
    bin_rstd = lax.rsqrt(stats[LEVELS : 2 * LEVELS] / counts - bin_mean * bin_mean + epsilon)
    normed = (pre - slot_rows(bin_mean)) * slot_rows(bin_rstd)
    gain, bias = own_half(branch_gain), own_half(branch_bias)
    feature, gelu_back = jax.vjp(jax.nn.gelu, slot_rows(gain) * normed + slot_rows(bias))
    feature = (mask[:, None] * feature).astype(BF16)
    features = feature
    other_features = swap_cores(features)
    if use_kernels:
        cell_w = cell_weights(me, branch_cols, of_slot, features, other_features, made[3])
    else:
        both = both_halves(features)
        cell_w = jnp.einsum("rbc,sc->brs", plain_cols(branch_cols), both, preferred_element_type=F32)
        cell_w = jnp.sum(cell_w * of_slot[:, None, :], axis=0).astype(BF16)
    cell_w = everyone(behind(cell_w, shares[1], shares[2]), "col")
    cell_w = cell_w.reshape(cols_n, TAPS, block_m, slots)
    cell_w = jnp.transpose(cell_w, (1, 0, 2, 3)).reshape(TAPS, half_mid, slots)

    other_cell_w = swap_cores(behind(cell_w, shares[3] if len(shares) > 3 else shares[-1]))
    if use_kernels:
        joined, head_sums = join_cells(me, up_views, cell_w, other_cell_w, shares, height, width)
    else:
        joined = sum(part.astype(F32) for part in shares)
        both_w = jnp.concatenate([jnp.where(first, cell_w, other_cell_w), jnp.where(first, other_cell_w, cell_w)], 1)
        for k in range(TAPS):
            view = up_views[:, k // 3 * width : (k // 3 + height) * width, k % 3 * slots : (k % 3 + 1) * slots]
            joined = joined + jnp.einsum("npq,mq->npm", view, both_w[k], preferred_element_type=F32)
        head_sums = jnp.stack([jnp.sum(joined, (0, 1)), jnp.sum(joined * joined, (0, 1))])
    joined = joined.reshape(own_pixels, mid)

    everywhere = ("row", "col", "img")
    head_sum = sum_over(head_sums, everywhere)
    head_mean = head_sum[0] / total_pixels
    head_rstd = lax.rsqrt(head_sum[1] / total_pixels - head_mean * head_mean + epsilon)
    normed_head = (joined - head_mean) * head_rstd
    activated, head_gelu_back = jax.vjp(jax.nn.gelu, join_gain * normed_head + join_bias)
    act_low = activated.astype(BF16)
    logits = lax.dot_general(class_w, act_low, (((0,), (1,)), ((), ())), preferred_element_type=F32)
    logits = logits + class_bias[:, None]
    row_peak = jnp.max(logits, axis=0, keepdims=True)
    exp_terms = jnp.exp(logits - row_peak)
    probabilities = exp_terms / jnp.sum(exp_terms, axis=0, keepdims=True)
    onehot = (labels.reshape(1, own_pixels) == jnp.arange(classes, dtype=jnp.int32)[:, None]).astype(F32)
    dlogits = ((probabilities - onehot) / math.sqrt(total_pixels)).astype(BF16)
    class_part = jnp.dot(dlogits, act_low, preferred_element_type=F32)
    class_bias_part = jnp.sum(dlogits.astype(F32), axis=1)
    grad_act = lax.dot_general(dlogits, class_w, (((0,), (1,)), ((), ())), preferred_element_type=F32)
    grad_head = head_gelu_back(grad_act)[0]
    everyone_n = rows_n * cols_n * img_n
    class_rows = jnp.concatenate([class_part, jnp.pad(class_bias_part, (0, mid - classes))[None]])
    row_block = -(-class_rows.shape[0] // everyone_n)
    class_rows = jnp.pad(class_rows, ((0, row_block * everyone_n - class_rows.shape[0]), (0, 0)))
    head_parts = jnp.stack([jnp.sum(grad_head, 0), jnp.sum(grad_head * normed_head, 0)])
    head_parts = jnp.broadcast_to(head_parts[None], (everyone_n, 2, mid))
    head_parts = jnp.concatenate([head_parts, class_rows.reshape(everyone_n, row_block, mid)], axis=1)
    head_totals = jnp.sum(exchange(head_parts, everywhere), axis=0)
    grad_join_bias, grad_join_gain = head_totals[0], head_totals[1]
    grad_joined = (
        join_gain * head_rstd * (grad_head - (grad_join_bias + normed_head * grad_join_gain) / total_pixels)
    ).astype(BF16).reshape(canvas_count, height, width, mid)

    left, right = edges(grad_joined)
    line = beside_row(grad_joined, left, right)
    own_g = jnp.concatenate([grad_joined.reshape(canvas_count, pixels, mid), left, right, line], axis=1)
    if img_n == 4:
        all_g = [own_g, partner(own_g, 1), partner(own_g, 2)]
        all_g.append(jnp.concatenate([partner(all_g[1][:1], 2), partner(all_g[2][1:], 1)]))
    else:
        all_g = [own_g] + [partner(own_g, s) for s in range(1, img_n)]

    by_pixel = []
    if use_kernels:
        back_parts = [None] * img_n

        def back_tile(s, *ahead):
            part, back_parts[s] = by_pixels(me, all_g[s], weights, height, width, BF16, ahead)
            by_pixel.append(part)

    else:
        grad_w = jnp.zeros((TAPS, depth, mid), F32)
        for s in range(img_n):
            part = jnp.zeros((canvas_count, pixels, depth), F32)
            grad_tap = []
            for k, window in enumerate(windows(all_g[s])[::-1]):
                part = part + jnp.einsum("npm,cm->npc", window, weights[k], preferred_element_type=F32)
                grad_tap.append(
                    jnp.einsum("npc,npm->cm", tiles[s][:, :pixels], window, preferred_element_type=F32)
                )
            grad_w = grad_w + jnp.stack(grad_tap)
            by_pixel.append(part if s == 0 else part.astype(BF16))
        grad_w = jnp.transpose(grad_w.astype(BF16).reshape(TAPS, cols_n, own_join, 2, half_mid), (3, 1, 0, 2, 4))
        grad_mine = lax.dynamic_index_in_dim(grad_w, row, 0, keepdims=False)
        grad_theirs = lax.dynamic_index_in_dim(grad_w, 1 - row, 0, keepdims=False)
        weights_token = back_token = jnp.zeros((8, 128), F32)
    if use_kernels:
        cell_grad, cell_send = cells_gradient(me, own_g, up_own, height, width)
    else:
        own_windows = windows(own_g)[::-1]
        cell_grad = jnp.stack(
            [
                jnp.einsum("npm,npq->mq", w, up_own, preferred_element_type=F32)
                for w in own_windows
            ]
        ).astype(BF16)
        cell_send = lax.dynamic_slice_in_dim(cell_grad, (1 - row) * half_mid, half_mid, 1)
        cell_grad = own_half(cell_grad, 1)

    if use_kernels:
        back_tile(0, cell_send)
    cell_grad = (cell_grad.astype(F32) + swap_cores(cell_send).astype(F32)).astype(BF16)
    cell_grad = jnp.transpose(cell_grad.reshape(TAPS, cols_n, block_m, slots), (1, 0, 2, 3))
    cell_grad = jnp.sum(exchange(cell_grad, "col").astype(F32), axis=0)
    if use_kernels:
        back_tile(1, back_parts[0])
        cell_grad = after(cell_grad, back_parts[1])
    cell_grad = cell_grad.astype(BF16)
    cell_grad = cell_grad.reshape(block_rows, slots)
    if use_kernels:
        branch_grad, feature_grad, feature_send = cell_back(
            me, branch_cols, of_slot, features, other_features, cell_grad
        )
    else:
        by_level = cell_grad[None] * of_slot.astype(BF16)[:, None, :]
        branch_grad = jnp.einsum("brs,sc->rbc", by_level, both, preferred_element_type=F32).astype(BF16)
        branch_grad = branch_grad.reshape(block_rows, cols_n, img_n, own_join)
        branch_grad = [
            jnp.transpose(lax.dynamic_index_in_dim(branch_grad, img ^ t, 2, keepdims=False), (1, 0, 2))
            for t in range(img_n)
        ]
        feature_grad = jnp.einsum("brs,rbc->sc", by_level, plain_cols(branch_cols), preferred_element_type=F32)
        feature_send = lax.dynamic_slice_in_dim(feature_grad, (1 - row) * half_mid, half_mid, 1).astype(BF16)
        feature_grad = own_half(feature_grad)
    feature_grad = (feature_grad + swap_cores(feature_send).astype(F32)).astype(BF16)

    if use_kernels:
        back_tile(2, back_parts[1])
    scattered = feature_grad.astype(BF16)
    if use_kernels:
        grad_theirs, weights_token = by_weights(
            me, False, all_g, flips, cols_n, height, width, [back_parts[2]]
        )
    feature_grad = scattered
    feature_grad = sum_over(feature_grad, "col")
    other_grad_w = swap_cores(grad_theirs)
    if use_kernels:
        grad_mine, weights_token = by_weights(me, True, all_g, flips, cols_n, height, width, [weights_token, scattered])
        feature_grad = after(feature_grad, weights_token)
        back_tile(3, weights_token, feature_grad)
        back_token = back_parts[3]

    by_pixel = [by_pixel[0]] + [partner(by_pixel[s], s) for s in range(1, img_n)]
    grad_main = (grad_mine.astype(F32) + other_grad_w.astype(F32)).astype(BF16)
    main_grads = ring_scatter(
        lambda t: lax.dynamic_index_in_dim(grad_main, (col - 1 - t) % cols_n, 0, keepdims=False), "col"
    )
    main_grad = jnp.transpose(main_grads[-1], (1, 0, 2))
    grad_y = gelu_back(feature_grad)[0]
    bin_totals = jnp.concatenate([level_sums(grad_y), level_sums(grad_y * normed)])
    bin_totals = sum_over(behind(bin_totals, grad_main), "img")
    correction = mask[:, None] * (
        slot_rows(bin_totals[:LEVELS] / counts) + normed * slot_rows(bin_totals[LEVELS:] / counts)
    )
    grad_pre = (slot_rows(gain) * slot_rows(bin_rstd) * (grad_y - correction)).astype(BF16)
    grad_pre = to_levels(both_halves(grad_pre))
    bin_totals = both_halves(bin_totals)
    grad_branch_bias, grad_branch_gain = bin_totals[:LEVELS], bin_totals[LEVELS:]

    weight_grad = lax.dot_general(
        pooled, grad_pre, (((0,), (0,)), ((), ())), preferred_element_type=F32
    ).astype(BF16)
    weight_grad = scatter(weight_grad.reshape(img_n, own_branch, LEVELS * mid), "img")

    grad_pooled = lax.dot_general(grad_pre, bw_rows, (((1,), (1,)), ((), ())), preferred_element_type=F32)
    grad_pooled = behind(grad_pooled / counted[:, None], main_grads[1], by_pixel[2]).astype(BF16)
    grad_pooled = jnp.transpose(everyone(grad_pooled, "col"), (1, 0, 2)).reshape(slots, half_channels)
    branch_grad = [part if t == 0 else partner(part, t) for t, part in enumerate(branch_grad)]
    branch_grad = sum(part.astype(F32) for part in branch_grad).astype(BF16)
    branch_grad = exchange(behind(branch_grad, grad_pooled), "col").reshape(cols_n, TAPS, block_m, own_join)
    branch_grad = jnp.transpose(branch_grad, (3, 1, 0, 2)).reshape(own_join, TAPS, half_mid)

    sent = swap_cores(jnp.where(first, branch_grad, main_grad))
    kept = jnp.where(first, main_grad, branch_grad)
    grad_join_w = jnp.concatenate([jnp.where(first, kept, sent), jnp.where(first, sent, kept)], axis=2).astype(F32)


    grad_pooled = both_halves(behind(grad_pooled, main_grads[2], by_pixel[3]))

    class_totals = everyone(behind(head_totals[2:], grad_pooled), everywhere).reshape(-1, mid)
    grad_class_w = class_totals[:classes].T
    grad_class_bias = class_totals[classes, :classes]

    pool_flat = pool_own.reshape(canvas_count, pixels, slots)
    if use_kernels:
        grad_canvases = finish_canvases(me, pool_flat, grad_pooled, by_pixel, cols_n)
    else:
        grad_canvases = jnp.einsum("npq,qc->npc", pool_flat, grad_pooled, preferred_element_type=F32)
        grad_canvases = grad_canvases.reshape(canvas_count, pixels, cols_n, img_n, own_join)
        for s, part in enumerate(by_pixel):
            spot = (0, 0, 0, img ^ s, 0)
            part = part.astype(F32).reshape(canvas_count, pixels, cols_n, 1, own_join)
            part = part + lax.dynamic_slice(grad_canvases, spot, part.shape)
            grad_canvases = lax.dynamic_update_slice(grad_canvases, part, spot)
    grad_canvases = grad_canvases.reshape(canvases.shape)

    grad_branch_w = sum(behind(part, grad_canvases).astype(F32) for part in weight_grad).reshape(own_branch, LEVELS, mid)
    logits = logits.T.reshape(canvas_count, height, width, classes)
    return (
        logits,
        grad_canvases,
        grad_branch_w,
        grad_branch_gain,
        grad_branch_bias,
        grad_join_w,
        grad_join_gain,
        grad_join_bias,
        grad_class_w,
        grad_class_bias,
    )


def solution(mesh):
    in_specs = (
        P("img", "row", "col", None),
        P("img"),
        P("img", "row", "col"),
        P(("row", "col", "img"), None, None),
        P(),
        P(),
        P(("row", "col", "img"), None, None),
        P(),
        P(),
        P(),
        P(),
    )
    out_specs = (
        P("img", "row", "col", None),
        P("img", "row", "col", None),
        P(("row", "col", "img"), None, None),
        P(),
        P(),
        P(("row", "col", "img"), None, None),
        P(),
        P(),
        P(),
        P(),
    )
    return jax.shard_map(
        per_device, mesh=mesh, in_specs=in_specs, out_specs=out_specs, check_vma=False
    )
```

```python
import functools
import math

import jax
import jax.numpy as jnp
import numpy as np
from jax import lax
from jax.experimental import pallas as pl
from jax.experimental.pallas import tpu as pltpu
from jax.sharding import PartitionSpec as P

SIDE = 64
bin_scales = (1, 2, 3, 6)
epsilon = 1e-05
LEVELS = len(bin_scales)
TAPS = 9
BF16 = jnp.bfloat16
F32 = jnp.float32


def slot_lists():
    rows = []
    for level, size in enumerate(bin_scales):
        rows += [(level, a, b, 0) for a in range(2 * size) for b in range(2 * size)]
    for level, size in enumerate(bin_scales):
        rows += [(level, a, b, 1) for a in range(size) for b in range(size)]
    rows += [(-1, 0, 0, 1)] * (-len(rows) % 128)
    return [np.array(column) for column in zip(*rows)]


def axis_tables(cell, level):
    size = np.array(bin_scales)[np.maximum(level, 0)][:, None]
    places = np.arange(SIDE)[None, :]
    pools, ups, valids = [], [], []
    for packed in (0, 1):
        image_side = SIDE // 2 if packed else SIDE
        which_half, in_cell = cell[:, None] // size, cell[:, None] % size
        pixel_half = places // image_side
        local_pos = places - pixel_half * image_side
        usable = ((which_half == 0) | (packed == 1)) & (level[:, None] >= 0)
        same_image = (pixel_half == which_half) & usable
        low_edge = in_cell * image_side // size
        high_edge = ((in_cell + 1) * image_side + size - 1) // size
        inside = same_image & (local_pos >= low_edge) & (local_pos < high_edge)
        numerator = local_pos * (size - 1)
        base_cell = numerator // (image_side - 1)
        fraction = (numerator - base_cell * (image_side - 1)).astype(np.float32) / np.float32(image_side - 1)
        weight = np.where(in_cell == base_cell, np.float32(1) - fraction, np.float32(0))
        weight = weight + np.where(in_cell == base_cell + 1, fraction, np.float32(0))
        weight = np.where(same_image, weight, np.float32(0)).astype(np.float32)
        pad = ((0, 0), (1, 1))
        pools.append(np.pad(inside.astype(np.float32), pad))
        ups.append(np.pad(weight, pad))
        valids.append(usable[:, 0].astype(np.float32))
    return np.stack(pools), np.stack(ups), np.stack(valids)


def swap_cores(x):
    return lax.ppermute(x, "row", [(0, 1), (1, 0)])


def exchange(blocks, axis):
    return lax.all_to_all(blocks, axis, 0, 0, tiled=True)


def everyone(x, axis):
    return exchange(jnp.broadcast_to(x[None], (lax.axis_size(axis),) + x.shape), axis)


def partner(x, step):
    count = lax.axis_size("img")
    return lax.ppermute(x, "img", [(a, a ^ step) for a in range(count)])


def scatter(blocks, axis):
    me, count = lax.axis_index(axis), lax.axis_size(axis)
    parts = [lax.dynamic_index_in_dim(blocks, me ^ s, 0, keepdims=False) for s in range(count)]
    return [parts[0]] + [
        lax.ppermute(parts[s], axis, [(a, a ^ s) for a in range(count)]) for s in range(1, count)
    ]


def sum_over(x, axis):
    return jnp.sum(everyone(x, axis).astype(F32), axis=0)


def ring_gather(x, axis):
    count = lax.axis_size(axis)
    parts = [x]
    for _ in range(count - 1):
        parts.append(lax.ppermute(parts[-1], axis, [(a, (a + 1) % count) for a in range(count)]))
    return parts


def ring_scatter(block_of, axis):
    count = lax.axis_size(axis)
    totals = [block_of(0)]
    for t in range(1, count):
        total = lax.ppermute(totals[-1], axis, [(a, (a + 1) % count) for a in range(count)])
        totals.append((total.astype(F32) + block_of(t).astype(F32)).astype(BF16))
    return totals


VMEM_LIMIT = 56 << 20


def cost(microseconds):
    return pl.CostEstimate(
        flops=int(microseconds * 10e9), bytes_accessed=int(microseconds * 32e6), transcendentals=0
    )


ANYWHERE = pl.BlockSpec(memory_space=pl.ANY)
BESIDE = 16 + 16


def whole(a, buffers=None):
    mode = {} if buffers is None else {"pipeline_mode": pl.Buffered(buffers)}
    return pl.BlockSpec(a.shape, lambda *_, r=len(a.shape): (0,) * r, **mode)


def pack_kernel(me, *refs, groups):
    sources, outs = refs[:4], refs[5:]
    lanes = outs[0].shape[2] // groups
    start = 0
    for ref in sources:
        size = ref.shape[1]
        for s, out_ref in enumerate(outs):
            for j in range(groups):
                at = pl.ds(pl.multiple_of((j * len(outs) + (me[2] ^ s)) * lanes, lanes), lanes)
                out_ref[0, start : start + size, j * lanes : (j + 1) * lanes] = ref[0, :, at]
        start += size


def pack(me, tile, left, right, line, blocks, groups, ahead):
    count, _, channels = tile.shape
    sources = (tile, left, right, line)
    rows = sum(x.shape[1] for x in sources)
    depth = channels // blocks
    return pl.pallas_call(
        functools.partial(pack_kernel, groups=groups),
        grid_spec=pltpu.PrefetchScalarGridSpec(
            num_scalar_prefetch=1,
            grid=(count,),
            in_specs=[pl.BlockSpec((1,) + x.shape[1:], lambda n, p: (n, 0, 0)) for x in sources] + [ANYWHERE],
            out_specs=[pl.BlockSpec((1, rows, depth), lambda n, p: (n, 0, 0))] * blocks,
        ),
        out_shape=[jax.ShapeDtypeStruct((count, rows, depth), tile.dtype)] * blocks,
        compiler_params=pltpu.CompilerParams(vmem_limit_bytes=VMEM_LIMIT),
        cost_estimate=cost(7.5),
        name="pack",
    )(me, *sources, ahead)


def lay_rows(rows_ref, wide_ref, row, pixels, left, right, beside, height, width):
    depth = rows_ref.shape[1] // 3
    rows = wide_ref.shape[0]
    for lane in range(0, depth, 128):
        at = slice(lane, lane + 128)
        edge = beside(0, width, at).astype(F32)
        corners = beside(width, 16, at).astype(F32)
        wide_ref[1 : height + 1, 8 : 8 + width] = pixels(at).astype(F32).reshape(height, width, 128)
        flat = wide_ref.reshape(rows * 32, 128)
        flat[pl.ds(32 + 7, height, stride=32)] = left(at).astype(F32)
        flat[pl.ds(32 + 8 + width, height, stride=32)] = right(at).astype(F32)
        for start, there in ((0, row == 1), ((height + 1) * 32, row == 0)):
            flat[start + 8 : start + 8 + width] = jnp.where(there, edge, 0.0)
            flat[start + 7 : start + 8] = jnp.where(there, corners[0:1], 0.0)
            flat[start + 8 + width : start + 9 + width] = jnp.where(there, corners[1:2], 0.0)
        for shift in range(3):
            view = wide_ref[:, 7 + shift : 7 + shift + width].reshape(rows * width, 128)
            rows_ref[:, shift * depth + lane : shift * depth + lane + 128] = view.astype(BF16)


def lay_tile(rows_ref, wide_ref, row, tile_ref, height, width):
    pixels = height * width

    def part(first, size):
        return lambda at: tile_ref[0, first : first + size, at]

    def beside(start, size, at):
        return tile_ref[0, pixels + 2 * height + start : pixels + 2 * height + start + size, at]

    lay_rows(
        rows_ref,
        wide_ref,
        row,
        part(0, pixels),
        part(pixels, height),
        part(pixels + height, height),
        beside,
        height,
        width,
    )


def wide_scratch(height):
    return pltpu.VMEM((height + 2, 32, 128), F32)


def join_kernel(me, x_ref, *refs, height, width, have, extra):
    if have:
        w_ref, (out_ref, flip_ref, rows_ref, wide_ref) = refs[0], refs[1 + extra :]
    else:
        mine_ref, theirs_ref = refs[:2]
        out_ref, flip_ref, w_ref, token_ref, rows_ref, wide_ref = refs[2 + extra :]
        groups, _, rows, half = mine_ref.shape

        @pl.when(pl.program_id(0) == 0)
        def _():
            token_ref[...] = jnp.zeros(token_ref.shape, F32)
            for t in range(groups):
                start = pl.multiple_of((me[1] + groups - t) % groups * rows, rows)
                for ref, side in ((mine_ref, me[0]), (theirs_ref, 1 - me[0])):
                    w_ref[:, pl.ds(start, rows), pl.ds(pl.multiple_of(side * half, half), half)] = ref[t]

    depth = x_ref.shape[-1]
    lay_tile(rows_ref, wide_ref, me[0], x_ref, height, width)
    flip_ref[0] = x_ref[0, : height * width].T
    total = jnp.zeros(out_ref.shape[1:], F32)
    for dy in range(3):
        total = total + jnp.dot(
            rows_ref[dy * width : (dy + height) * width],
            w_ref[3 * dy : 3 * dy + 3].reshape(3 * depth, -1),
            preferred_element_type=F32,
        )
    out_ref[0] = total.astype(out_ref.dtype)


def join_tiles(me, x, weights, height, width, dtype, ahead=()):
    count, _, depth = x.shape
    pixels = height * width
    have = not isinstance(weights, tuple)
    if have:
        weights = (weights,)
        taps, m = weights[0].shape[0], weights[0].shape[2]
    else:
        taps, m = weights[0].shape[1], 2 * weights[0].shape[3]
    out = jax.ShapeDtypeStruct((count, pixels, m), dtype)
    made = jax.ShapeDtypeStruct((taps, depth, m), BF16)
    token = jax.ShapeDtypeStruct((8, 128), F32)
    flip = jax.ShapeDtypeStruct((count, depth, pixels), BF16)
    out_spec = [
        pl.BlockSpec((1, pixels, m), lambda n, p: (n, 0, 0)),
        pl.BlockSpec((1, depth, pixels), lambda n, p: (n, 0, 0)),
    ]
    return pl.pallas_call(
        functools.partial(join_kernel, height=height, width=width, have=have, extra=len(ahead)),
        grid_spec=pltpu.PrefetchScalarGridSpec(
            num_scalar_prefetch=1,
            grid=(count,),
            in_specs=[pl.BlockSpec((1,) + x.shape[1:], lambda n, p: (n, 0, 0))]
            + [whole(w, 1) for w in weights]
            + [ANYWHERE] * len(ahead),
            out_specs=out_spec + ([] if have else [whole(made, 1), whole(token)]),
            scratch_shapes=[pltpu.VMEM(((height + 2) * width, 3 * depth), BF16), wide_scratch(height)],
        ),
        out_shape=[out, flip] + ([] if have else [made, token]),
        compiler_params=pltpu.CompilerParams(vmem_limit_bytes=VMEM_LIMIT),
        cost_estimate=cost(4),
        name="join_tiles",
    )(me, x, *weights, *ahead)


def cells_kernel(me, up_ref, mine_ref, theirs_ref, *refs, height, width):
    parts, (out_ref, sums_ref) = refs[:-2], refs[-2:]
    slots = mine_ref.shape[2]
    half = mine_ref.shape[1]
    for ref, side in ((mine_ref, me[0]), (theirs_ref, 1 - me[0])):
        total = jnp.zeros((height * width, half), F32)
        for k in range(TAPS):
            dy, dx = k // 3, k % 3
            total = total + lax.dot_general(
                up_ref[0, dy * width : (dy + height) * width, dx * slots : (dx + 1) * slots],
                ref[k],
                (((1,), (1,)), ((), ())),
                preferred_element_type=F32,
            )
        out_ref[0, :, pl.ds(pl.multiple_of(side * half, half), half)] = total
    total = out_ref[0]
    for part_ref in parts:
        total = total + part_ref[0].astype(F32)
    out_ref[0] = total

    @pl.when(pl.program_id(0) == 0)
    def _():
        sums_ref[...] = jnp.zeros(sums_ref.shape, F32)

    sums_ref[0:1] += jnp.sum(total, 0, keepdims=True)
    sums_ref[1:2] += jnp.sum(total * total, 0, keepdims=True)


def join_cells(me, up, mine, theirs, parts, height, width):
    count, pixels, m = parts[0].shape
    return pl.pallas_call(
        functools.partial(cells_kernel, height=height, width=width),
        grid_spec=pltpu.PrefetchScalarGridSpec(
            num_scalar_prefetch=1,
            grid=(count,),
            in_specs=[pl.BlockSpec((1,) + up.shape[1:], lambda n, p: (n, 0, 0)), whole(mine), whole(theirs)]
            + [pl.BlockSpec((1, pixels, m), lambda n, p: (n, 0, 0))] * len(parts),
            out_specs=[
                pl.BlockSpec((1, pixels, m), lambda n, p: (n, 0, 0)),
                pl.BlockSpec((2, m), lambda n, p: (0, 0)),
            ],
        ),
        out_shape=[jax.ShapeDtypeStruct((count, pixels, m), F32), jax.ShapeDtypeStruct((2, m), F32)],
        compiler_params=pltpu.CompilerParams(vmem_limit_bytes=VMEM_LIMIT),
        cost_estimate=cost(2.25),
        name="join_cells",
    )(me, up, mine, theirs, *parts)


def tap_rows(rows_ref, k, height, width):
    m = rows_ref.shape[1] // 3
    dy, dx = 2 - k // 3, 2 - k % 3
    return rows_ref[dy * width : (dy + height) * width, dx * m : (dx + 1) * m]


def cells_back_kernel(me, g_ref, up_ref, mine_ref, theirs_ref, total_ref, rows_ref, wide_ref, *, height, width):
    lay_tile(rows_ref, wide_ref, me[0], g_ref, height, width)
    half = mine_ref.shape[1]
    count = pl.num_programs(0)
    cells = up_ref[0].T

    @pl.when(pl.program_id(0) == 0)
    def _():
        total_ref[...] = jnp.zeros(total_ref.shape, F32)

    for k in range(TAPS):
        total_ref[k] += jnp.dot(cells, tap_rows(rows_ref, k, height, width), preferred_element_type=F32)

    @pl.when(pl.program_id(0) == count - 1)
    def _():
        for k in range(TAPS):
            for ref, side in ((mine_ref, me[0]), (theirs_ref, 1 - me[0])):
                ref[k] = total_ref[k, :, pl.ds(pl.multiple_of(side * half, half), half)].T.astype(BF16)


def cells_gradient(me, g, up, height, width):
    count, rows, m = g.shape
    slots = up.shape[2]
    out = jax.ShapeDtypeStruct((TAPS, m // 2, slots), BF16)
    return pl.pallas_call(
        functools.partial(cells_back_kernel, height=height, width=width),
        grid_spec=pltpu.PrefetchScalarGridSpec(
            num_scalar_prefetch=1,
            grid=(count,),
            in_specs=[
                pl.BlockSpec((1, rows, m), lambda n, p: (n, 0, 0)),
                pl.BlockSpec((1,) + up.shape[1:], lambda n, p: (n, 0, 0)),
            ],
            out_specs=[whole(out), whole(out)],
            scratch_shapes=[
                pltpu.VMEM((TAPS, slots, m), F32),
                pltpu.VMEM(((height + 2) * width, 3 * m), BF16),
                wide_scratch(height),
            ],
        ),
        out_shape=[out, out],
        compiler_params=pltpu.CompilerParams(vmem_limit_bytes=VMEM_LIMIT),
        cost_estimate=cost(6),
        name="cells_gradient",
    )(me, g, up)


def by_pixels_kernel(me, g_ref, w_ref, *refs, height, width):
    dx_ref, token_ref, rows_ref, wide_ref = refs[-4:]
    lay_tile(rows_ref, wide_ref, me[0], g_ref, height, width)
    token_ref[...] = jnp.zeros(token_ref.shape, F32)
    total = jnp.zeros(dx_ref.shape[1:], F32)
    for k in range(TAPS):
        total = total + lax.dot_general(
            tap_rows(rows_ref, k, height, width), w_ref[k], (((1,), (1,)), ((), ())), preferred_element_type=F32
        )
    dx_ref[0] = total.astype(dx_ref.dtype)


def by_pixels(me, g, weights, height, width, dtype, ahead=()):
    count, rows, m = g.shape
    depth = weights.shape[1]
    return pl.pallas_call(
        functools.partial(by_pixels_kernel, height=height, width=width),
        grid_spec=pltpu.PrefetchScalarGridSpec(
            num_scalar_prefetch=1,
            grid=(count,),
            in_specs=[pl.BlockSpec((1, rows, m), lambda n, p: (n, 0, 0)), whole(weights, 1)]
            + [ANYWHERE] * len(ahead),
            out_specs=[
                pl.BlockSpec((1, height * width, depth), lambda n, p: (n, 0, 0)),
                pl.BlockSpec((8, 128), lambda n, p: (0, 0)),
            ],
            scratch_shapes=[pltpu.VMEM(((height + 2) * width, 3 * m), BF16), wide_scratch(height)],
        ),
        out_shape=[
            jax.ShapeDtypeStruct((count, height * width, depth), dtype),
            jax.ShapeDtypeStruct((8, 128), F32),
        ],
        compiler_params=pltpu.CompilerParams(vmem_limit_bytes=VMEM_LIMIT),
        cost_estimate=cost(6.3),
        name="by_pixels",
    )(me, g, weights, *ahead)


def by_weights_kernel(me, *refs, height, width, tiles):
    g_refs, x_refs = refs[:tiles], refs[tiles : 2 * tiles]
    out_ref, token_ref, rows_ref, wide_ref, x_ref, total_ref = refs[-6:]
    step = pl.program_id(0)
    count = g_refs[0].shape[0]
    pixels = height * width
    for s in range(tiles):

        @pl.when(step == s)
        def _(s=s):
            for n in range(count):
                lay_tile(rows_ref.at[n], wide_ref, me[0], g_refs[s].at[pl.ds(n, 1)], height, width)
                x_ref[:, n * pixels : (n + 1) * pixels] = x_refs[s][n]

    @pl.when(step == 0)
    def _():
        total_ref[...] = jnp.zeros(total_ref.shape, F32)

    for k in range(TAPS):
        for n in range(count):
            total_ref[k] += jnp.dot(
                x_ref[:, n * pixels : (n + 1) * pixels],
                tap_rows(rows_ref.at[n], k, height, width),
                preferred_element_type=F32,
            )

    @pl.when(step == tiles - 1)
    def _():
        token_ref[...] = jnp.zeros(token_ref.shape, F32)
        groups, _, rows, _ = out_ref.shape
        for j in range(groups):
            out_ref[j] = total_ref[:, j * rows : (j + 1) * rows].astype(BF16)


def by_weights(me, own, gs, xs, groups, height, width, ahead=()):
    tiles = len(gs)
    count, rows, m = gs[0].shape
    depth = xs[0].shape[1]
    out = jax.ShapeDtypeStruct((groups, TAPS, depth // groups, m // 2), BF16)
    token = jax.ShapeDtypeStruct((8, 128), F32)
    half = pl.BlockSpec(
        (count, rows, m // 2), lambda s, p: (0, 0, p[0] if own else 1 - p[0]), pipeline_mode=pl.Buffered(1)
    )
    return pl.pallas_call(
        functools.partial(by_weights_kernel, height=height, width=width, tiles=tiles),
        grid_spec=pltpu.PrefetchScalarGridSpec(
            num_scalar_prefetch=1,
            grid=(tiles,),
            in_specs=[half] * tiles + [whole(x, 1) for x in xs] + [ANYWHERE] * len(ahead),
            out_specs=[whole(out, 1), whole(token)],
            scratch_shapes=[
                pltpu.VMEM((count, (height + 2) * width, 3 * m // 2), BF16),
                wide_scratch(height),
                pltpu.VMEM((depth, count * height * width), BF16),
                pltpu.VMEM((TAPS, depth, m // 2), F32),
            ],
        ),
        out_shape=[out, token],
        compiler_params=pltpu.CompilerParams(vmem_limit_bytes=VMEM_LIMIT),
        cost_estimate=cost(20),
        name="by_weights",
    )(me, *gs, *xs, *ahead)


def finish_kernel(me, pool_ref, cells_ref, *refs, groups):
    parts, out_ref, sum_ref = refs[:-2], refs[-2], refs[-1]
    lanes = parts[0].shape[2] // groups
    for s, ref in enumerate(parts):
        for j in range(groups):
            at = pl.ds(pl.multiple_of((j * len(parts) + (me[2] ^ s)) * lanes, lanes), lanes)
            sum_ref[:, at] = ref[0, :, j * lanes : (j + 1) * lanes]
    depth = parts[0].shape[2]
    for c in range(0, out_ref.shape[2], depth):
        at = slice(c, c + depth)
        out_ref[0, :, at] = sum_ref[:, at].astype(F32) + jnp.dot(
            pool_ref[0], cells_ref[:, at], preferred_element_type=F32
        )


def finish_canvases(me, pool, cells, parts, groups):
    count, pixels, slots = pool.shape
    channels = cells.shape[1]
    return pl.pallas_call(
        functools.partial(finish_kernel, groups=groups),
        grid_spec=pltpu.PrefetchScalarGridSpec(
            num_scalar_prefetch=1,
            grid=(count,),
            in_specs=[pl.BlockSpec((1, pixels, slots), lambda n, p: (n, 0, 0)), whole(cells)]
            + [pl.BlockSpec((1,) + part.shape[1:], lambda n, p: (n, 0, 0)) for part in parts],
            out_specs=pl.BlockSpec((1, pixels, channels), lambda n, p: (n, 0, 0)),
            scratch_shapes=[pltpu.VMEM((pixels, channels), BF16)],
        ),
        out_shape=jax.ShapeDtypeStruct((count, pixels, channels), F32),
        compiler_params=pltpu.CompilerParams(vmem_limit_bytes=VMEM_LIMIT),
        cost_estimate=cost(8),
        name="finish_canvases",
    )(me, pool, cells, *parts)


def all_features(me, feat_ref, mine_ref, theirs_ref):
    half = mine_ref.shape[1]
    for ref, side in ((mine_ref, me[0]), (theirs_ref, 1 - me[0])):
        feat_ref[:, pl.ds(pl.multiple_of(side * half, half), half)] = ref[...]


def cell_weights_kernel(me, level_ref, mine_ref, theirs_ref, *refs, parts):
    cols, (out_ref, feat_ref) = refs[:parts], refs[-2:]
    all_features(me, feat_ref, mine_ref, theirs_ref)
    total = jnp.zeros(out_ref.shape, F32)
    for b in range(LEVELS):
        part = jnp.zeros(out_ref.shape, F32)
        for t, ref in enumerate(cols):
            lanes = ref.shape[2]
            feat = feat_ref[:, pl.ds(pl.multiple_of((me[2] ^ t) * lanes, lanes), lanes)]
            part = part + lax.dot_general(ref[b], feat, (((1,), (1,)), ((), ())), preferred_element_type=F32)
        total = total + level_ref[b : b + 1, :] * part
    out_ref[...] = total.astype(BF16)


def cell_weights(me, cols, of_slot, mine, theirs, ahead):
    slots, half = mine.shape
    out = jax.ShapeDtypeStruct((cols[0].shape[1], slots), BF16)
    return pl.pallas_call(
        functools.partial(cell_weights_kernel, parts=len(cols)),
        grid_spec=pltpu.PrefetchScalarGridSpec(
            num_scalar_prefetch=1,
            grid=(1,),
            in_specs=[whole(of_slot), whole(mine), whole(theirs)] + [whole(c) for c in cols] + [ANYWHERE],
            out_specs=whole(out),
            scratch_shapes=[pltpu.VMEM((slots, 2 * half), BF16)],
        ),
        out_shape=out,
        compiler_params=pltpu.CompilerParams(vmem_limit_bytes=VMEM_LIMIT),
        cost_estimate=cost(4),
        name="cell_weights",
    )(me, of_slot, mine, theirs, *cols, ahead)


def cell_back_kernel(me, level_ref, mine_ref, theirs_ref, grad_ref, *refs, parts):
    cols, col_grads = refs[:parts], refs[parts : 2 * parts]
    own_ref, send_ref, feat_ref, back_ref = refs[2 * parts :]
    all_features(me, feat_ref, mine_ref, theirs_ref)
    half = mine_ref.shape[1]
    grads = [grad_ref[...] * level_ref[b : b + 1, :].astype(BF16) for b in range(LEVELS)]
    for t, (ref, out_ref) in enumerate(zip(cols, col_grads)):
        lanes = ref.shape[2]
        at = pl.ds(pl.multiple_of((me[2] ^ t) * lanes, lanes), lanes)
        total = jnp.zeros((mine_ref.shape[0], lanes), F32)
        for b in range(LEVELS):
            out_ref[b] = jnp.dot(grads[b], feat_ref[:, at], preferred_element_type=F32).astype(BF16)
            total = total + lax.dot_general(
                grads[b], ref[b], (((0,), (0,)), ((), ())), preferred_element_type=F32
            )
        back_ref[:, at] = total
    for ref, side in ((own_ref, me[0]), (send_ref, 1 - me[0])):
        ref[...] = back_ref[:, pl.ds(pl.multiple_of(side * half, half), half)].astype(ref.dtype)


def cell_back(me, cols, of_slot, mine, theirs, grad):
    slots, half = mine.shape
    outs = [jax.ShapeDtypeStruct(c.shape, BF16) for c in cols]
    outs += [jax.ShapeDtypeStruct(mine.shape, F32), jax.ShapeDtypeStruct(mine.shape, BF16)]
    *col_grads, own, send = pl.pallas_call(
        functools.partial(cell_back_kernel, parts=len(cols)),
        grid_spec=pltpu.PrefetchScalarGridSpec(
            num_scalar_prefetch=1,
            grid=(1,),
            in_specs=[whole(a) for a in (of_slot, mine, theirs, grad)] + [whole(c) for c in cols],
            out_specs=[whole(a) for a in outs],
            scratch_shapes=[pltpu.VMEM((slots, 2 * half), BF16), pltpu.VMEM((slots, 2 * half), F32)],
        ),
        out_shape=outs,
        compiler_params=pltpu.CompilerParams(vmem_limit_bytes=VMEM_LIMIT),
        cost_estimate=cost(5),
        name="cell_back",
    )(me, of_slot, mine, theirs, grad, *cols)
    return col_grads, own, send


def per_device(
    canvases,
    layout,
    labels,
    branch_w,
    branch_gain,
    branch_bias,
    join_w,
    join_gain,
    join_bias,
    class_w,
    class_bias,
):
    canvas_count, height, width, channels = canvases.shape
    mid = join_w.shape[2]
    half_mid = mid // 2
    classes = class_w.shape[1]
    own_join = join_w.shape[0]
    own_branch = branch_w.shape[0]
    row, col, img = lax.axis_index("row"), lax.axis_index("col"), lax.axis_index("img")
    rows_n, cols_n, img_n = lax.axis_size("row"), lax.axis_size("col"), lax.axis_size("img")
    tall = height * rows_n
    pixels = height * width
    own_pixels = canvas_count * pixels
    total_pixels = own_pixels * rows_n * cols_n * img_n
    devices = cols_n * img_n
    group = row * cols_n + col
    group_c = channels // (rows_n * cols_n)
    depth = channels // img_n
    first = row == 0
    use_kernels = width == 16 and height % 16 == 0 and own_join % 128 == 0 and img_n == 4

    def own_half(x, axis=-1):
        return lax.dynamic_slice_in_dim(x, row * half_mid, half_mid, axis)

    def both_halves(x, axis=-1):
        other = swap_cores(x)
        return jnp.concatenate([jnp.where(first, x, other), jnp.where(first, other, x)], axis=axis)

    taps_first = jnp.transpose(join_w, (1, 0, 2))
    kept = own_half(taps_first)
    swapped = swap_cores(lax.dynamic_slice_in_dim(taps_first, (1 - row) * half_mid, half_mid, 2))
    main_w = jnp.where(first, kept, swapped)
    branch_part = jnp.where(first, swapped, kept)

    me = jnp.stack([row, col, img]).astype(jnp.int32)

    def after(x, token):
        return x + token[0, 0].astype(x.dtype)

    def behind(x, *others):
        if not others:
            return x
        return x + sum((other[(0,) * other.ndim] * 0).astype(F32) for other in others).astype(x.dtype)

    ends = cols_n - 1
    left = lax.ppermute(canvases[:, :, -1], "col", [(a, a + 1) for a in range(ends)])
    right = lax.ppermute(canvases[:, :, 0], "col", [(a + 1, a) for a in range(ends)])
    shards_list = ring_gather(behind(main_w, left, right), "col")
    shards = jnp.stack(shards_list)

    def edges(tile):
        left = lax.ppermute(tile[:, :, -1], "col", [(a, a + 1) for a in range(ends)])
        right = lax.ppermute(tile[:, :, 0], "col", [(a + 1, a) for a in range(ends)])
        return left, right

    def beside_row(tile, left, right):
        edge = jnp.where(first, height - 1, 0)
        line = lax.dynamic_index_in_dim(tile, edge, 1, keepdims=False)
        corners = [lax.dynamic_slice_in_dim(side, edge, 1, 1) for side in (left, right)]
        line = jnp.concatenate([line] + corners + [jnp.zeros_like(line[:, :1])] * (BESIDE - width - 2), axis=1)
        return swap_cores(line)

    def windows(tile):
        left, right = (tile[:, pixels + k * height : pixels + (k + 1) * height] for k in range(2))
        line = tile[:, pixels + 2 * height :]
        tile = tile[:, :pixels].reshape(-1, height, width, tile.shape[2])
        wide = jnp.concatenate([left[:, :, None], tile, right[:, :, None]], axis=2)
        line = jnp.concatenate([line[:, width : width + 1], line[:, :width], line[:, width + 1 : width + 2]], axis=1)
        line = line[:, None]
        wide = jnp.concatenate([jnp.where(first, 0, line), wide, jnp.where(first, line, 0)], axis=1)
        return [
            wide[:, k // 3 : k // 3 + height, k % 3 : k % 3 + width].reshape(-1, pixels, wide.shape[3])
            for k in range(TAPS)
        ]

    surround = (canvases.reshape(canvas_count, pixels, channels), left, right, beside_row(canvases, left, right))
    if use_kernels:
        tiles = pack(me, *surround, img_n, cols_n, main_w)
    else:
        by_block = jnp.concatenate(surround, axis=1).reshape(canvas_count, -1, cols_n, img_n, own_join)
        tiles = [
            lax.dynamic_index_in_dim(by_block, img ^ s, 3, keepdims=False).reshape(canvas_count, -1, depth)
            for s in range(img_n)
        ]
    packed = tiles[0]
    tiles = [packed] + [partner(tiles[s], s) for s in range(1, img_n)]

    other_shards = swap_cores(behind(shards, *tiles[1:3]))

    if not use_kernels:
        weights = jnp.zeros((TAPS, cols_n, own_join, 2, half_mid), BF16)
        for t in range(cols_n):
            for shard, side in ((shards[t], row), (other_shards[t], 1 - row)):
                spot = (0, (col - t) % cols_n, 0, side, 0)
                weights = lax.dynamic_update_slice(weights, shard[:, None, :, None], spot)
        weights = weights.reshape(TAPS, depth, mid)
    shares, made, flips = [], [], []
    for s in range(img_n):
        dtype = F32 if s == 0 else BF16
        if use_kernels and s == 0:
            share, flip, weights, token = join_tiles(me, tiles[s], (shards, other_shards), height, width, dtype)
            flips.append(flip)
        elif use_kernels:
            share, flip = join_tiles(me, tiles[s], weights, height, width, dtype)
            flips.append(flip)
        else:
            share = jnp.zeros((canvas_count, pixels, mid), F32)
            for k, window in enumerate(windows(tiles[s])):
                share = share + jnp.einsum("npc,cm->npm", window, weights[k], preferred_element_type=F32)
            share = share.astype(dtype)
            token = jnp.zeros((8, 128), F32)
        made.append(share)
        shares.append(share if s == 0 else partner(share, s))

    bw_rows = everyone(behind(branch_w.reshape(own_branch, LEVELS * mid), main_w), "img")
    bw_rows = bw_rows.reshape(group_c, LEVELS * mid)


    slot_level, slot_a, slot_b, slot_second = slot_lists()
    slots = len(slot_level)
    tables = [np.concatenate(axis_tables(c, slot_level)[:2], 2) for c in (slot_a, slot_b)]
    valid = axis_tables(slot_a, slot_level)[2] * axis_tables(slot_b, slot_level)[2]
    counts = [np.sum(axis_tables(c, slot_level)[0], 2) for c in (slot_a, slot_b)]
    counts = np.maximum(counts[0] * counts[1], 1)
    tables = np.concatenate(tables + [valid[:, :, None], counts[:, :, None]], 2).astype(np.float32)
    tables = np.where((slot_second == 1)[None, :, None], tables[:1], tables)
    may_pack = jnp.where(layout[0] == 1, 0, 1)
    tables = behind(jnp.where(layout[may_pack] == 1, tables[1], tables[0]), packed, shards_list[2], bw_rows)
    span = SIDE + 2
    pool_rows, up_rows, pool_cols, up_cols = (tables[:, k * span : (k + 1) * span] for k in range(4))
    mask, counted = tables[:, 4 * span], tables[:, 4 * span + 1]
    on_canvas = jnp.asarray(slot_second)[None, :] == (may_pack != jnp.arange(canvas_count))[:, None]
    on_canvas = on_canvas.astype(F32)
    of_slot = jnp.asarray((slot_level[None, :] == np.arange(LEVELS)[:, None]).astype(np.float32))
    level_mask = of_slot * mask

    def pixel_table(rows, cols):
        table = rows.T[None, :, None, :] * cols.T[None, None, :, :]
        return (on_canvas[:, None, None, :] * table).astype(BF16)

    def own_rows(table, margin):
        return lax.dynamic_slice_in_dim(table, 1 + row * height - margin, height + 2 * margin, 1)

    near_cols = lax.dynamic_slice_in_dim(up_cols, col * width, width + 2, 1)
    up_views = jnp.concatenate(
        [pixel_table(own_rows(up_rows, 1), near_cols[:, dx : dx + width]) for dx in range(3)], axis=3
    ).reshape(canvas_count, (height + 2) * width, 3 * slots)
    up_own = pixel_table(own_rows(up_rows, 0), near_cols[:, 1:-1]).reshape(canvas_count, pixels, slots)
    pool_own = pixel_table(
        own_rows(pool_rows, 0),
        lax.dynamic_slice_in_dim(pool_cols, 1 + col * width, width, 1),
    )

    pool_part = jnp.einsum("nyxq,nyxc->qc", pool_own, canvases, preferred_element_type=F32)
    half_channels = channels // rows_n
    mine = lax.dynamic_slice_in_dim(pool_part, row * half_channels, half_channels, 1)
    mine = mine + swap_cores(lax.dynamic_slice_in_dim(pool_part, (1 - row) * half_channels, half_channels, 1))
    mine = behind(mine, shards_list[-1])
    mine = jnp.transpose(mine.astype(BF16).reshape(slots, cols_n, group_c), (1, 0, 2))
    pool_sums = jnp.sum(exchange(mine, "col").astype(F32), axis=0)
    block_m = half_mid // cols_n
    block_rows = TAPS * block_m
    by_column = jnp.transpose(branch_part, (0, 2, 1)).reshape(TAPS, cols_n, block_m, own_join)
    by_column = jnp.transpose(by_column, (1, 0, 2, 3)).reshape(cols_n, block_rows, own_join)
    by_column = exchange(behind(by_column, pool_sums), "col")
    branch_cols = [by_column] + [partner(by_column, t) for t in range(1, img_n)]

    def plain_cols(parts):
        out = jnp.zeros((img_n,) + parts[0].shape, parts[0].dtype)
        for t, part in enumerate(parts):
            out = lax.dynamic_update_slice(out, part[None], (img ^ t, 0, 0, 0))
        return jnp.transpose(out, (2, 1, 0, 3)).reshape(block_rows, LEVELS, mid)

    pool_sums = after(pool_sums, token)
    pooled = (pool_sums / counted[:, None]).astype(BF16)

    def of_level(wide):
        k = wide.shape[1] // LEVELS
        return sum(of_slot[b][:, None] * wide[:, b * k : (b + 1) * k] for b in range(LEVELS))

    def to_levels(narrow):
        return jnp.concatenate([of_slot[b][:, None].astype(narrow.dtype) * narrow for b in range(LEVELS)], axis=1)

    def slot_rows(per_level):
        return sum(of_slot[b][:, None] * per_level[b][None] for b in range(LEVELS))

    def level_sums(per_slot):
        return jnp.stack([jnp.sum(level_mask[b][:, None] * per_slot, axis=0) for b in range(LEVELS)])

    pre_part = of_level(jnp.dot(pooled, bw_rows, preferred_element_type=F32))
    pre = own_half(pre_part) + swap_cores(lax.dynamic_slice_in_dim(pre_part, (1 - row) * half_mid, half_mid, 1))
    pre = sum_over(behind(pre, by_column).astype(BF16), "col")
    pre = behind(pre, made[1])
    count_part = jnp.broadcast_to(jnp.sum(level_mask, 1)[:, None], (LEVELS, half_mid))
    stats = sum_over(jnp.concatenate([level_sums(pre), level_sums(pre * pre), count_part]), "img")
    stats = behind(stats, made[2], tiles[3])
    counts = stats[2 * LEVELS :]
    bin_mean = stats[:LEVELS] / counts
    bin_rstd = lax.rsqrt(stats[LEVELS : 2 * LEVELS] / counts - bin_mean * bin_mean + epsilon)
    normed = (pre - slot_rows(bin_mean)) * slot_rows(bin_rstd)
    gain, bias = own_half(branch_gain), own_half(branch_bias)
    feature, gelu_back = jax.vjp(jax.nn.gelu, slot_rows(gain) * normed + slot_rows(bias))
    feature = (mask[:, None] * feature).astype(BF16)
    features = feature
    other_features = swap_cores(features)
    if use_kernels:
        cell_w = cell_weights(me, branch_cols, of_slot, features, other_features, made[3])
    else:
        both = both_halves(features)
        cell_w = jnp.einsum("rbc,sc->brs", plain_cols(branch_cols), both, preferred_element_type=F32)
        cell_w = jnp.sum(cell_w * of_slot[:, None, :], axis=0).astype(BF16)
    cell_w = everyone(behind(cell_w, shares[1], shares[2]), "col")
    cell_w = cell_w.reshape(cols_n, TAPS, block_m, slots)
    cell_w = jnp.transpose(cell_w, (1, 0, 2, 3)).reshape(TAPS, half_mid, slots)

    other_cell_w = swap_cores(behind(cell_w, shares[3] if len(shares) > 3 else shares[-1]))
    if use_kernels:
        joined, head_sums = join_cells(me, up_views, cell_w, other_cell_w, shares, height, width)
    else:
        joined = sum(part.astype(F32) for part in shares)
        both_w = jnp.concatenate([jnp.where(first, cell_w, other_cell_w), jnp.where(first, other_cell_w, cell_w)], 1)
        for k in range(TAPS):
            view = up_views[:, k // 3 * width : (k // 3 + height) * width, k % 3 * slots : (k % 3 + 1) * slots]
            joined = joined + jnp.einsum("npq,mq->npm", view, both_w[k], preferred_element_type=F32)
        head_sums = jnp.stack([jnp.sum(joined, (0, 1)), jnp.sum(joined * joined, (0, 1))])
    joined = joined.reshape(own_pixels, mid)

    everywhere = ("row", "col", "img")
    head_sum = sum_over(head_sums, everywhere)
    head_mean = head_sum[0] / total_pixels
    head_rstd = lax.rsqrt(head_sum[1] / total_pixels - head_mean * head_mean + epsilon)
    normed_head = (joined - head_mean) * head_rstd
    activated, head_gelu_back = jax.vjp(jax.nn.gelu, join_gain * normed_head + join_bias)
    act_low = activated.astype(BF16)
    logits = lax.dot_general(class_w, act_low, (((0,), (1,)), ((), ())), preferred_element_type=F32)
    logits = logits + class_bias[:, None]
    row_peak = jnp.max(logits, axis=0, keepdims=True)
    exp_terms = jnp.exp(logits - row_peak)
    probabilities = exp_terms / jnp.sum(exp_terms, axis=0, keepdims=True)
    onehot = (labels.reshape(1, own_pixels) == jnp.arange(classes, dtype=jnp.int32)[:, None]).astype(F32)
    dlogits = ((probabilities - onehot) / math.sqrt(total_pixels)).astype(BF16)
    class_part = jnp.dot(dlogits, act_low, preferred_element_type=F32)
    class_bias_part = jnp.sum(dlogits.astype(F32), axis=1)
    grad_act = lax.dot_general(dlogits, class_w, (((0,), (1,)), ((), ())), preferred_element_type=F32)
    grad_head = head_gelu_back(grad_act)[0]
    everyone_n = rows_n * cols_n * img_n
    class_rows = jnp.concatenate([class_part, jnp.pad(class_bias_part, (0, mid - classes))[None]])
    row_block = -(-class_rows.shape[0] // everyone_n)
    class_rows = jnp.pad(class_rows, ((0, row_block * everyone_n - class_rows.shape[0]), (0, 0)))
    head_parts = jnp.stack([jnp.sum(grad_head, 0), jnp.sum(grad_head * normed_head, 0)])
    head_parts = jnp.broadcast_to(head_parts[None], (everyone_n, 2, mid))
    head_parts = jnp.concatenate([head_parts, class_rows.reshape(everyone_n, row_block, mid)], axis=1)
    head_totals = jnp.sum(exchange(head_parts, everywhere), axis=0)
    grad_join_bias, grad_join_gain = head_totals[0], head_totals[1]
    grad_joined = (
        join_gain * head_rstd * (grad_head - (grad_join_bias + normed_head * grad_join_gain) / total_pixels)
    ).astype(BF16).reshape(canvas_count, height, width, mid)

    left, right = edges(grad_joined)
    line = beside_row(grad_joined, left, right)
    own_g = jnp.concatenate([grad_joined.reshape(canvas_count, pixels, mid), left, right, line], axis=1)
    if img_n == 4:
        all_g = [own_g, partner(own_g, 1), partner(own_g, 2)]
        all_g.append(jnp.concatenate([partner(all_g[1][:1], 2), partner(all_g[2][1:], 1)]))
    else:
        all_g = [own_g] + [partner(own_g, s) for s in range(1, img_n)]

    by_pixel = []
    if use_kernels:
        back_parts = [None] * img_n

        def back_tile(s, *ahead):
            part, back_parts[s] = by_pixels(me, all_g[s], weights, height, width, BF16, ahead)
            by_pixel.append(part)

    else:
        grad_w = jnp.zeros((TAPS, depth, mid), F32)
        for s in range(img_n):
            part = jnp.zeros((canvas_count, pixels, depth), F32)
            grad_tap = []
            for k, window in enumerate(windows(all_g[s])[::-1]):
                part = part + jnp.einsum("npm,cm->npc", window, weights[k], preferred_element_type=F32)
                grad_tap.append(
                    jnp.einsum("npc,npm->cm", tiles[s][:, :pixels], window, preferred_element_type=F32)
                )
            grad_w = grad_w + jnp.stack(grad_tap)
            by_pixel.append(part if s == 0 else part.astype(BF16))
        grad_w = jnp.transpose(grad_w.astype(BF16).reshape(TAPS, cols_n, own_join, 2, half_mid), (3, 1, 0, 2, 4))
        grad_mine = lax.dynamic_index_in_dim(grad_w, row, 0, keepdims=False)
        grad_theirs = lax.dynamic_index_in_dim(grad_w, 1 - row, 0, keepdims=False)
        weights_token = back_token = jnp.zeros((8, 128), F32)
    if use_kernels:
        cell_grad, cell_send = cells_gradient(me, own_g, up_own, height, width)
    else:
        own_windows = windows(own_g)[::-1]
        cell_grad = jnp.stack(
            [
                jnp.einsum("npm,npq->mq", w, up_own, preferred_element_type=F32)
                for w in own_windows
            ]
        ).astype(BF16)
        cell_send = lax.dynamic_slice_in_dim(cell_grad, (1 - row) * half_mid, half_mid, 1)
        cell_grad = own_half(cell_grad, 1)

    if use_kernels:
        back_tile(0, cell_send)
    cell_grad = (cell_grad.astype(F32) + swap_cores(cell_send).astype(F32)).astype(BF16)
    cell_grad = jnp.transpose(cell_grad.reshape(TAPS, cols_n, block_m, slots), (1, 0, 2, 3))
    cell_grad = jnp.sum(exchange(cell_grad, "col").astype(F32), axis=0)
    if use_kernels:
        back_tile(1, back_parts[0])
        cell_grad = after(cell_grad, back_parts[1])
    cell_grad = cell_grad.astype(BF16)
    cell_grad = cell_grad.reshape(block_rows, slots)
    if use_kernels:
        branch_grad, feature_grad, feature_send = cell_back(
            me, branch_cols, of_slot, features, other_features, cell_grad
        )
    else:
        by_level = cell_grad[None] * of_slot.astype(BF16)[:, None, :]
        branch_grad = jnp.einsum("brs,sc->rbc", by_level, both, preferred_element_type=F32).astype(BF16)
        branch_grad = branch_grad.reshape(block_rows, cols_n, img_n, own_join)
        branch_grad = [
            jnp.transpose(lax.dynamic_index_in_dim(branch_grad, img ^ t, 2, keepdims=False), (1, 0, 2))
            for t in range(img_n)
        ]
        feature_grad = jnp.einsum("brs,rbc->sc", by_level, plain_cols(branch_cols), preferred_element_type=F32)
        feature_send = lax.dynamic_slice_in_dim(feature_grad, (1 - row) * half_mid, half_mid, 1).astype(BF16)
        feature_grad = own_half(feature_grad)
    feature_grad = (feature_grad + swap_cores(feature_send).astype(F32)).astype(BF16)

    if use_kernels:
        back_tile(2, back_parts[1])
    scattered = feature_grad.astype(BF16)
    if use_kernels:
        grad_theirs, weights_token = by_weights(
            me, False, all_g, flips, cols_n, height, width, [back_parts[2]]
        )
    feature_grad = scattered
    feature_grad = sum_over(feature_grad, "col")
    other_grad_w = swap_cores(grad_theirs)
    if use_kernels:
        grad_mine, weights_token = by_weights(me, True, all_g, flips, cols_n, height, width, [weights_token, scattered])
        feature_grad = after(feature_grad, weights_token)
        back_tile(3, weights_token, feature_grad)
        back_token = back_parts[3]

    by_pixel = [by_pixel[0]] + [partner(by_pixel[s], s) for s in range(1, img_n)]
    grad_main = (grad_mine.astype(F32) + other_grad_w.astype(F32)).astype(BF16)
    main_grads = ring_scatter(
        lambda t: lax.dynamic_index_in_dim(grad_main, (col - 1 - t) % cols_n, 0, keepdims=False), "col"
    )
    main_grad = jnp.transpose(main_grads[-1], (1, 0, 2))
    grad_y = gelu_back(feature_grad)[0]
    bin_totals = jnp.concatenate([level_sums(grad_y), level_sums(grad_y * normed)])
    bin_totals = sum_over(behind(bin_totals, grad_main), "img")
    correction = mask[:, None] * (
        slot_rows(bin_totals[:LEVELS] / counts) + normed * slot_rows(bin_totals[LEVELS:] / counts)
    )
    grad_pre = (slot_rows(gain) * slot_rows(bin_rstd) * (grad_y - correction)).astype(BF16)
    grad_pre = to_levels(both_halves(grad_pre))
    bin_totals = both_halves(bin_totals)
    grad_branch_bias, grad_branch_gain = bin_totals[:LEVELS], bin_totals[LEVELS:]

    weight_grad = lax.dot_general(
        pooled, grad_pre, (((0,), (0,)), ((), ())), preferred_element_type=F32
    ).astype(BF16)
    weight_grad = scatter(weight_grad.reshape(img_n, own_branch, LEVELS * mid), "img")

    grad_pooled = lax.dot_general(grad_pre, bw_rows, (((1,), (1,)), ((), ())), preferred_element_type=F32)
    grad_pooled = behind(grad_pooled / counted[:, None], main_grads[1], by_pixel[2]).astype(BF16)
    grad_pooled = jnp.transpose(everyone(grad_pooled, "col"), (1, 0, 2)).reshape(slots, half_channels)
    branch_grad = [part if t == 0 else partner(part, t) for t, part in enumerate(branch_grad)]
    branch_grad = sum(part.astype(F32) for part in branch_grad).astype(BF16)
    branch_grad = exchange(behind(branch_grad, grad_pooled), "col").reshape(cols_n, TAPS, block_m, own_join)
    branch_grad = jnp.transpose(branch_grad, (3, 1, 0, 2)).reshape(own_join, TAPS, half_mid)

    sent = swap_cores(jnp.where(first, branch_grad, main_grad))
    kept = jnp.where(first, main_grad, branch_grad)
    grad_join_w = jnp.concatenate([jnp.where(first, kept, sent), jnp.where(first, sent, kept)], axis=2).astype(F32)


    grad_pooled = both_halves(behind(grad_pooled, main_grads[2], by_pixel[3]))

    class_totals = everyone(behind(head_totals[2:], grad_pooled), everywhere).reshape(-1, mid)
    grad_class_w = class_totals[:classes].T
    grad_class_bias = class_totals[classes, :classes]

    pool_flat = pool_own.reshape(canvas_count, pixels, slots)
    if use_kernels:
        grad_canvases = finish_canvases(me, pool_flat, grad_pooled, by_pixel, cols_n)
    else:
        grad_canvases = jnp.einsum("npq,qc->npc", pool_flat, grad_pooled, preferred_element_type=F32)
        grad_canvases = grad_canvases.reshape(canvas_count, pixels, cols_n, img_n, own_join)
        for s, part in enumerate(by_pixel):
            spot = (0, 0, 0, img ^ s, 0)
            part = part.astype(F32).reshape(canvas_count, pixels, cols_n, 1, own_join)
            part = part + lax.dynamic_slice(grad_canvases, spot, part.shape)
            grad_canvases = lax.dynamic_update_slice(grad_canvases, part, spot)
    grad_canvases = grad_canvases.reshape(canvases.shape)

    grad_branch_w = sum(behind(part, grad_canvases).astype(F32) for part in weight_grad).reshape(own_branch, LEVELS, mid)
    logits = logits.T.reshape(canvas_count, height, width, classes)
    return (
        logits,
        grad_canvases,
        grad_branch_w,
        grad_branch_gain,
        grad_branch_bias,
        grad_join_w,
        grad_join_gain,
        grad_join_bias,
        grad_class_w,
        grad_class_bias,
    )


def solution(mesh):
    in_specs = (
        P("img", "row", "col", None),
        P("img"),
        P("img", "row", "col"),
        P(("row", "col", "img"), None, None),
        P(),
        P(),
        P(("row", "col", "img"), None, None),
        P(),
        P(),
        P(),
        P(),
    )
    out_specs = (
        P("img", "row", "col", None),
        P("img", "row", "col", None),
        P(("row", "col", "img"), None, None),
        P(),
        P(),
        P(("row", "col", "img"), None, None),
        P(),
        P(),
        P(),
        P(),
    )
    return jax.shard_map(
        per_device, mesh=mesh, in_specs=in_specs, out_specs=out_specs, check_vma=False
    )
```
